256 devices in a mesh: blk: 4 (over x), seq: 16 (over z, core), tensor: 4 (over y).
Axes of the slice: x: 4, y: 4, z: 8, core: 2. Of those that a mesh axis runs over, the one named last changes fastest.
Arguments:
- tokens: bfloat16 [4, 4096, 4096], P('blk', 'seq', 'tensor'), may hold values from -20 to 20
- w_query: bfloat16 [4, 4096, 2048], P('blk', 'seq', 'tensor'), may hold values from -0.09375 to 0.09375
- w_keyval: bfloat16 [4, 4096, 4, 256], P('blk', 'seq', 'tensor'), may hold values from -0.09375 to 0.09375
- accum_query: float32 [4, 4096, 2048], P('blk', 'seq', 'tensor'), may hold values from -0.75 to 0.75
- accum_keyval: float32 [4, 4096, 4, 256], P('blk', 'seq', 'tensor'), may hold values from -0.75 to 0.75
- cotangent: bfloat16 [4, 4096, 2048], P('blk', 'seq', 'tensor'), may hold values from -6 to 6
- seg_ids: int32 [4, 4096], P('blk'), may hold values from 0 to 7, never falling along the last dimension, each value on 1 to 2048 neighbouring positions
- spans: int32 [4, 8, 2], P('blk'), may hold values from 0 to 4096, as said below
- counts: int32 [4, 16], P('blk'), may hold values from 128 to 256, as said below
Outputs:
- context: bfloat16 [4, 4096, 2048], P('blk', 'seq', 'tensor')
- grad_tokens: bfloat16 [4, 4096, 4096], P('blk', 'seq', 'tensor')
- accum_query_out: float32 [4, 4096, 2048], P('blk', 'seq', 'tensor')
- accum_keyval_out: float32 [4, 4096, 4, 256], P('blk', 'seq', 'tensor')
The draws below stay inside these ranges and needn't reach their ends.
Inputs may be any that keep to these rules, and one draw needn't show every extreme that they name: `spans`: start < end for every document slot; some slot starts at 0 and some ends at 4096 in every micro-batch. `counts`: in every micro-batch some index of seq is full.
All inputs are finite; a program needn't handle non-finite values.
Results may differ from the reference program's by a relative error of at most 0.011.
Values may be sent and summed in bfloat16 or wider, within the bound.
A program may use at most 128 MiB of HBM per device.

```python
import math
import jax
import jax.numpy as jnp
import numpy as np
from jax import lax

D = 4096
H = 16
KEY_VALUE_HEADS = 4
HEAD_SIZE = 128
MB_DEV = 256
SEGS = 8
BLOCKS = 4
MICRO_TOKENS = 4096
N_SEQ = 16


def draw_tokens(key, part):
    key = jax.random.fold_in(key, 11)
    first = jax.random.fold_in(key, 0)
    value_rows = jnp.clip(jax.random.normal(first, (BLOCKS, MICRO_TOKENS, D), jnp.float32), -6.0, 6.0)
    return value_rows.astype(jnp.bfloat16)


def draw_spans(key, part):
    key = jax.random.fold_in(key, 23)
    first, second = jax.random.split(key)
    starts = jax.random.randint(first, (BLOCKS, SEGS), 0, MICRO_TOKENS - 1)
    widths = jax.random.randint(second, (BLOCKS, SEGS), 1, MICRO_TOKENS // 2 + 1)
    slot = jnp.arange(SEGS, dtype=jnp.int32)[None, :]
    starts = jnp.where(slot == 0, 0, starts)
    ends = jnp.minimum(starts + widths, MICRO_TOKENS)
    ends = jnp.where(slot == SEGS - 1, MICRO_TOKENS, ends)
    return jnp.stack([starts, ends], axis=-1).astype(jnp.int32)


def draw_counts(key, part):
    key = jax.random.fold_in(key, 37)
    first, second = jax.random.split(key)
    value_rows = jax.random.randint(first, (BLOCKS, N_SEQ), MB_DEV // 2, MB_DEV + 1)
    full_at = jax.random.randint(second, (BLOCKS, 1), 0, N_SEQ)
    lanes = jnp.arange(N_SEQ, dtype=jnp.int32)[None, :]
    return jnp.where(lanes == full_at, MB_DEV, value_rows).astype(jnp.int32)


def level_of(key, extent, pieces, low, top_value):
    def one(position, shards_of):
        heights = jax.random.uniform(jax.random.fold_in(jax.random.fold_in(key, 6), position), (shards_of,), jnp.float32, low / len(pieces), top_value / len(pieces))
        return jnp.repeat(jnp.exp(heights), extent[position] // shards_of).reshape((-1,) + (1,) * (len(extent) - position - 1))

    factor_of = one(*pieces[0])
    for cut in pieces[1:]:
        factor_of = factor_of * one(*cut)
    return factor_of


def length_profile(number_of, total, limit, slope):
    portions = [(1 << 20) // math.isqrt(grade ** slope) + 1 for grade in range(2, number_of + 1)]
    spare, holding = total - limit - (number_of - 1), [1] * (number_of - 1)
    while spare > 0:
        movable = [i for i in range(number_of - 1) if holding[i] < limit]
        mass, budget = sum([portions[i] for i in movable]), spare
        for i in movable:
            addition = min(limit - holding[i], max(1, budget * portions[i] // mass), spare)
            holding[i] = holding[i] + addition
            spare = spare - addition
    return np.array([limit] + holding)


def ragged_sizes(own_key, count, total, bound, lean):
    if count == 2:
        one = jax.random.randint(own_key, (), max(1, total - bound), min(bound, total - 1) + 1)
        return jnp.stack([one, total - one])
    sizes = jnp.asarray(length_profile(count, total, bound, lean), jnp.int32)
    twos = (count - 1) // 2
    giver, receiver = sizes[1:1 + 2 * twos:2], sizes[2:2 + 2 * twos:2]
    room = jnp.minimum(giver - 1, bound - receiver)
    shifted = jax.random.randint(jax.random.fold_in(own_key, 1), (twos,), 0, 1 << 20) % (room + 1)
    sizes = sizes.at[1:1 + 2 * twos:2].set(giver - shifted).at[2:2 + 2 * twos:2].set(receiver + shifted)
    return sizes[jax.random.permutation(jax.random.fold_in(own_key, 2), count)]


def gaussian(key, shape, width, reach, pieces=(), kind=jnp.bfloat16):
    values = jax.random.normal(key, shape, jnp.float32) * width
    if len(pieces) > 0:
        values = level_of(key, shape, pieces, -0.22, 0.18) * values
    return jnp.clip(values, min=-reach, max=reach).astype(kind)


def setup_inputs(seed: int = 0) -> dict:
    streams_of = jax.random.split(jax.random.key(seed), 10)
    tokens = draw_tokens(jax.random.fold_in(streams_of[9], 71), 0)
    w_query = gaussian(streams_of[1], (BLOCKS, D, H * HEAD_SIZE), D ** -0.5, 0.09375, ((0, 4), (1, 16), (2, 4)))
    w_keyval = gaussian(streams_of[2], (BLOCKS, D, KEY_VALUE_HEADS, 2 * HEAD_SIZE), D ** -0.5, 0.09375, ((0, 4), (1, 16), (2, 4)))
    accum_query = gaussian(streams_of[3], (BLOCKS, D, H * HEAD_SIZE), 0.05, 0.75, ((0, 4), (1, 16), (2, 4)), jnp.float32)
    accum_keyval = gaussian(streams_of[4], (BLOCKS, D, KEY_VALUE_HEADS, 2 * HEAD_SIZE), 0.05, 0.75, ((0, 4), (1, 16), (2, 4)), jnp.float32)
    cotangent = gaussian(streams_of[5], (BLOCKS, MICRO_TOKENS, H * HEAD_SIZE), 1.0, 6.0, ((0, 4), (1, 16), (2, 4)))
    seg_ids = jax.vmap(lambda own: jnp.searchsorted(jnp.cumsum(ragged_sizes(own, SEGS, MICRO_TOKENS, MICRO_TOKENS // 2, 2)), jnp.arange(MICRO_TOKENS), side="right"))(jax.random.split(streams_of[6], BLOCKS)).reshape((BLOCKS, MICRO_TOKENS)).astype(jnp.int32)
    spans = draw_spans(jax.random.fold_in(streams_of[9], 71), 0)
    counts = draw_counts(jax.random.fold_in(streams_of[9], 71), 0)
    return {"tokens": tokens, "w_query": w_query, "w_keyval": w_keyval, "accum_query": accum_query, "accum_keyval": accum_keyval, "cotangent": cotangent, "seg_ids": seg_ids, "spans": spans, "counts": counts}


def one_batch(x, wq, wkv, output_cotangent, seg, span, cnt):
    query_per_group = H // KEY_VALUE_HEADS
    scale = HEAD_SIZE ** -0.5
    query = jnp.dot(x, wq, preferred_element_type=jnp.float32).astype(jnp.bfloat16)
    keyval = jnp.dot(x, wkv.reshape(D, KEY_VALUE_HEADS * 2 * HEAD_SIZE), preferred_element_type=jnp.float32).astype(jnp.bfloat16)
    qf = query.astype(jnp.float32).reshape(MICRO_TOKENS, KEY_VALUE_HEADS, query_per_group, HEAD_SIZE)
    kvf = keyval.astype(jnp.float32).reshape(MICRO_TOKENS, KEY_VALUE_HEADS, 2 * HEAD_SIZE)
    keyf = kvf[:, :, :HEAD_SIZE]
    value_float = kvf[:, :, HEAD_SIZE:]
    pos = jnp.arange(MICRO_TOKENS, dtype=jnp.int32)
    owner = jnp.repeat(cnt, MB_DEV, total_repeat_length=MICRO_TOKENS)
    pair_validity = (pos % MB_DEV) < owner
    onehot = seg[:, None] == jnp.arange(SEGS, dtype=jnp.int32)[None, :]
    first = jnp.sum(jnp.where(onehot, span[None, :, 0], 0), axis=1)
    last = jnp.sum(jnp.where(onehot, span[None, :, 1], 0), axis=1)
    inside = (pos >= first) & (pos < last)
    allowed = (seg[:, None] == seg[None, :]) & ((pos[None, :] <= pos[:, None]) | (inside[:, None] & inside[None, :])) & pair_validity[None, :]
    allowed = allowed | (pos[None, :] == pos[:, None])
    scores = jnp.einsum('igxd,jgd->gxij', qf, keyf) * scale
    scores = jnp.where(allowed[None, None], scores, -jnp.inf)
    top = jnp.max(scores, axis=-1, keepdims=True)
    expo = jnp.exp(scores - top)
    probs = expo / jnp.sum(expo, axis=-1, keepdims=True)
    probability_lowprec = probs.astype(jnp.bfloat16).astype(jnp.float32)
    value_mask = pair_validity.astype(jnp.float32)[:, None, None, None]
    attended_output = jnp.einsum('zcft,tzn->fzcn', probability_lowprec, value_float) * value_mask
    context = attended_output.reshape(MICRO_TOKENS, H * HEAD_SIZE).astype(jnp.bfloat16)
    upstream_gradient = output_cotangent.astype(jnp.float32).reshape(MICRO_TOKENS, KEY_VALUE_HEADS, query_per_group, HEAD_SIZE) * value_mask
    delta = jnp.transpose(jnp.sum(upstream_gradient * attended_output, axis=-1), (1, 2, 0))
    dprobs = jnp.einsum('igxd,jgd->gxij', upstream_gradient, value_float)
    dscores = (probs * (dprobs - delta[..., None]) * scale).astype(jnp.bfloat16).astype(jnp.float32)
    dquery = jnp.einsum('zcft,tzn->fzcn', dscores, keyf).astype(jnp.bfloat16).reshape(MICRO_TOKENS, H * HEAD_SIZE)
    dkey = jnp.einsum('gxij,igxd->jgd', dscores, qf)
    dval = jnp.einsum('gxij,igxd->jgd', probability_lowprec, upstream_gradient)
    dkeyval = jnp.concatenate([dkey, dval], axis=-1).astype(jnp.bfloat16).reshape(MICRO_TOKENS, KEY_VALUE_HEADS * 2 * HEAD_SIZE)
    grads = jnp.dot(dquery, wq.T, preferred_element_type=jnp.float32)
    grads = grads + jnp.dot(dkeyval, wkv.reshape(D, KEY_VALUE_HEADS * 2 * HEAD_SIZE).T, preferred_element_type=jnp.float32)
    grad_x = grads.astype(jnp.bfloat16)
    fresh_q = jnp.dot(x.T, dquery, preferred_element_type=jnp.float32) / MICRO_TOKENS
    fresh_kv = jnp.dot(x.T, dkeyval, preferred_element_type=jnp.float32) / MICRO_TOKENS
    return context, grad_x, fresh_q, fresh_kv.reshape(D, KEY_VALUE_HEADS, 2 * HEAD_SIZE)


def reference(tokens, w_query, w_keyval, accum_query, accum_keyval, cotangent, seg_ids, spans, counts):
    used_q = jnp.roll(w_query, 1, axis=0)
    used_kv = jnp.roll(w_keyval, 1, axis=0)
    context, grad_tokens, fresh_q, fresh_kv = lax.map(lambda a: one_batch(*a), (tokens, used_q, used_kv, cotangent, seg_ids, spans, counts))
    accum_query_out = jnp.roll(accum_query, 1, axis=0) + jnp.roll(fresh_q, -1, axis=0)
    accum_keyval_out = jnp.roll(accum_keyval, 1, axis=0) + jnp.roll(fresh_kv, -1, axis=0)
    return context, grad_tokens, accum_query_out, accum_keyval_out
```

```python
import functools

import jax
import jax.numpy as jnp
from jax import lax
from jax.experimental import pallas as pl
from jax.experimental.pallas import tpu as pltpu
from jax.sharding import PartitionSpec as P

MESH = pl.DeviceIdType.MESH
BF16 = jnp.bfloat16
F32 = jnp.float32
MIB = 1 << 20
LOG2E = 1.4426950408889634
MASKED = -1e30


def matmul(a, b):
    return jnp.dot(a, b, preferred_element_type=F32)


def matmul_t(a, b):
    return lax.dot_general(a, b, (((1,), (1,)), ((), ())), preferred_element_type=F32)


class Place:
    def __init__(self, n_blk, n_seq, n_tensor):
        self.n_blk, self.chips, self.n_tensor = n_blk, n_seq // 2, n_tensor
        me = lax.axis_index("seq")
        self.core, self.chip = lax.rem(me, 2), lax.div(me, 2)
        self.blk, self.t = lax.axis_index("blk"), lax.axis_index("tensor")
        self.sibling = {"seq": me + 1 - 2 * self.core}

    def at(self, distance):
        return lax.rem(self.chip + distance + self.chips, self.chips)

    def along_seq(self, distance):
        return {"seq": 2 * self.at(distance) + self.core}

    def along_blk(self, distance):
        return {"blk": lax.rem(self.blk + distance + self.n_blk, self.n_blk)}

    def tensor_at(self, distance):
        return lax.rem(self.t + distance + self.n_tensor, self.n_tensor)

    def along_tensor(self, distance):
        return {"tensor": self.tensor_at(distance)}

    def greet(self):
        barrier = pltpu.get_barrier_semaphore()
        others = [self.sibling]
        for sign in (1, -1):
            others += [self.along_seq(sign), self.along_blk(sign), self.along_tensor(sign)]
        for other in others:
            pl.semaphore_signal(barrier, inc=1, device_id=other, device_id_type=MESH)
        pl.semaphore_wait(barrier, len(others))


class Links:
    def __init__(self, send, recv):
        self.send, self.recv, self.used, self.sent = send, recv, 0, []

    def copy(self, src, dst, to, arrives=None):
        i = self.used
        self.used += 1
        made = pltpu.make_async_remote_copy(
            src_ref=src, dst_ref=dst, send_sem=self.send.at[i], recv_sem=self.recv.at[i],
            device_id=to, device_id_type=MESH,
        )
        landing = made
        if arrives is not None:
            landing = pltpu.make_async_remote_copy(
                src_ref=arrives, dst_ref=arrives, send_sem=self.send.at[i], recv_sem=self.recv.at[i],
                device_id=to, device_id_type=MESH,
            )
        made.start()
        self.sent.append(made)
        return landing.wait_recv

    def drain(self):
        for made in self.sent:
            made.wait_send()


def gather_kernel(
    sizes, tok, wq, wkv, x2t_out, wq_out, wkv_out, kv_out, q_out,
    xb, x2t, xts, wqb, wkvb, kvb, send, recv, local,
):
    place = Place(*sizes)
    links = Links(send, recv)
    chips, half = place.chips, place.chips // 2
    rows = tok.shape[0]
    krows = wq.shape[0]
    sub = krows // 2
    halves = (pl.ds(0, sub), pl.ds(sub, sub))
    full = pl.ds(0, krows)
    c = place.core

    own_tok = pltpu.make_async_copy(tok, xb.at[place.t], local.at[0])
    own_tok.start()
    place.greet()

    def pass_on(buf, sign, step, part):
        src = buf.at[place.at(-sign * (step - 1)), c, part]
        return links.copy(src, src, place.along_seq(sign), buf.at[place.at(-sign * step), c, part])

    def both_ways(buf, step):
        parts = (full, full) if step < half else halves
        waits = [pass_on(buf, sign, step, part) for sign, part in zip((1, -1), parts)]
        return lambda: [w() for w in waits]

    def half_ways(buf, step, h):
        signs = [s for i, s in enumerate((1, -1)) if step < half or i == h]
        waits = [pass_on(buf, sign, step, halves[h]) for sign in signs]
        return lambda: [w() for w in waits]

    shared = {}

    def share(buf, key, distance):
        src = buf.at[place.at(distance), c]
        got = links.copy(src, src, place.sibling, buf.at[place.at(distance), 1 - c])
        shared.setdefault(key, []).append(got)

    def share_step(buf, key, step):
        for distance in (step, -step) if step < half else (step,):
            share(buf, key, distance)

    def collect(key):
        for got in shared[key]:
            got()

    ahead = place.along_blk(1)
    slot = place.chip
    shift_kv = links.copy(wkv, wkvb.at[slot, c], ahead)
    shift_q = [
        links.copy(wq.at[h], wqb.at[slot, c, h], ahead) for h in halves
    ]
    up = links.copy(tok, xb.at[place.t], place.along_tensor(1), xb.at[place.tensor_at(-1)])
    down = links.copy(tok, xb.at[place.t], place.along_tensor(-1), xb.at[place.tensor_at(1)])

    shift_kv()
    kv_got = both_ways(wkvb, 1)
    share(wkvb, "kv", 0)
    shift_q[0]()
    q_got = [half_ways(wqb, 1, 0), None]
    kv_got()
    kv_got = both_ways(wkvb, 2)
    share_step(wkvb, "kv", 1)
    shift_q[1]()
    q_got[1] = half_ways(wqb, 1, 1)
    share(wqb, "q", 0)

    up()
    rsub = rows // 2
    near = (pl.ds(0, rsub), pl.ds(rsub, rsub))
    src = xb.at[place.tensor_at(-1), near[0]]
    up_far = links.copy(src, src, place.along_tensor(1), xb.at[place.tensor_at(-2), near[0]])
    down()
    src = xb.at[place.tensor_at(1), near[1]]
    down_far = links.copy(src, src, place.along_tensor(-1), xb.at[place.tensor_at(2), near[1]])

    q_step = [1, 1]

    def advance_q(h):
        if q_got[h] is None:
            return
        q_got[h]()
        q_got[h] = None
        done = q_step[h]
        if done < half:
            q_step[h] += 1
            q_got[h] = half_ways(wqb, q_step[h], h)
        if h == 1 and done < half:
            share_step(wqb, "q", done)

    for step in range(2, half + 1):
        kv_got()
        if step < half:
            kv_got = both_ways(wkvb, step + 1)
        share_step(wkvb, "kv", step)
        if step < half:
            advance_q(step % 2)
    up_far()
    down_far()
    own_tok.wait()
    per = chips // sizes[2]
    collect("kv")
    keyval = None
    for t in range(sizes[2]):
        part = wkvb[t * per:(t + 1) * per].reshape(2 * per * krows, wkv.shape[1])
        term = matmul(xb[t], part)
        keyval = term if keyval is None else keyval + term
    kvb[place.chip, c] = keyval.astype(BF16)
    kv_got = both_ways(kvb, 1)
    share(kvb, "all", 0)
    save_kv = pltpu.make_async_copy(wkvb, wkv_out, local.at[1])
    save_kv.start()

    def turn(i):
        for p in range(per):
            zz = i * per + p
            mine = pl.ds(pl.multiple_of((2 * p + c) * krows, krows), krows)
            other = pl.ds(pl.multiple_of((2 * p + 1 - c) * krows, krows), krows)
            x2t[zz, :, :rows] = xb[i, :, mine].T
            xts[zz] = xb[i, :, other].T

    turns = list(range(sizes[2]))
    for step in range(1, half + 1):
        advance_q(0)
        advance_q(1)
        if turns:
            turn(turns.pop(0))
        kv_got()
        if step < half:
            kv_got = both_ways(kvb, step + 1)
        share_step(kvb, "all", step)
    while turns:
        turn(turns.pop(0))
    x_got = links.copy(
        xts, x2t.at[:, :, pl.ds(rows, rows)], place.sibling
    )
    while q_got[0] is not None or q_got[1] is not None:
        advance_q(0)
        advance_q(1)
    share(wqb, "q", half)
    collect("q")
    save_q = pltpu.make_async_copy(wqb, wq_out, local.at[2])
    save_q.start()
    query = None
    for t in range(sizes[2]):
        part = wqb[t * per:(t + 1) * per].reshape(2 * per * krows, wq.shape[1])
        term = matmul(xb[t], part)
        query = term if query is None else query + term
    q_out[...] = query.astype(BF16)
    collect("all")
    save_all = pltpu.make_async_copy(kvb, kv_out, local.at[3])
    save_all.start()
    x_got()
    save_x = pltpu.make_async_copy(x2t, x2t_out, local.at[4])
    save_x.start()
    links.drain()
    for save in (save_kv, save_q, save_all, save_x):
        save.wait()


def gather_project(sizes, tok, wq, wkv):
    n_blk, n_seq, n_tensor = sizes
    chips = n_seq // 2
    rows, krows, qcols, kcols = tok.shape[0], wq.shape[0], wq.shape[1], wkv.shape[1]
    hbm = pl.BlockSpec(memory_space=pl.ANY)
    shapes = [
        jax.ShapeDtypeStruct((chips, krows, 2 * rows), BF16),
        jax.ShapeDtypeStruct((chips, 2, krows, qcols), BF16),
        jax.ShapeDtypeStruct((chips, 2, krows, kcols), BF16),
        jax.ShapeDtypeStruct((chips, 2, rows, kcols), BF16),
        jax.ShapeDtypeStruct((rows, qcols), BF16),
    ]
    return pl.pallas_call(
        functools.partial(gather_kernel, sizes),
        out_shape=shapes,
        in_specs=[hbm] * 3,
        out_specs=[hbm] * 4 + [pl.BlockSpec(memory_space=pltpu.VMEM)],
        scratch_shapes=[
            pltpu.VMEM((n_tensor,) + tok.shape, BF16),
            pltpu.VMEM(shapes[0].shape, BF16),
            pltpu.VMEM((chips, krows, rows), BF16),
            pltpu.VMEM(shapes[1].shape, BF16),
            pltpu.VMEM(shapes[2].shape, BF16),
            pltpu.VMEM(shapes[3].shape, BF16),
            pltpu.SemaphoreType.DMA((100,)),
            pltpu.SemaphoreType.DMA((100,)),
            pltpu.SemaphoreType.DMA((5,)),
        ],
        compiler_params=pltpu.CompilerParams(
            collective_id=0, has_side_effects=True, vmem_limit_bytes=48 * MIB
        ),
        name="gather_project",
    )(tok, wq, wkv)


def attention_kernel(
    heads, me, span, counts, seg, query, kv, cot, ctx, dquery, dkv,
    s_buf, e_buf, qt, ut, o_acc, dq_acc,
):
    rows = query.shape[0]
    hs = query.shape[1] // heads
    blocks = kv.shape[0]
    total = blocks * rows
    slots = span.shape[0] // 2
    rank = me[0]
    c = hs ** -0.5 * LOG2E

    seg_all = seg[...]
    seg_q = seg[pl.ds(rank, 1), :]
    qpos = rank * rows + lax.broadcasted_iota(jnp.int32, (1, rows), 1)
    lo = jnp.zeros((1, rows), jnp.int32)
    hi = jnp.zeros((1, rows), jnp.int32)
    begin = jnp.int32(0)
    for s in range(slots):
        end = jnp.sum((seg_all <= s).astype(F32)).astype(jnp.int32)
        first, last = span[2 * s], span[2 * s + 1]
        here = seg_q == s
        inside = (qpos >= first) & (qpos < last)
        lo = jnp.where(here, begin, lo)
        hi = jnp.where(here, jnp.where(inside, jnp.minimum(last, end), qpos + 1), hi)
        begin = end
    b_lo = lax.div(jnp.min(lo.astype(F32)).astype(jnp.int32), rows)
    b_hi = lax.div(jnp.max(hi.astype(F32)).astype(jnp.int32) + rows - 1, rows)
    valid_t = lax.broadcasted_iota(jnp.int32, (1, rows), 1) < counts[rank]

    dkv[...] = jnp.zeros_like(dkv)
    o_acc[...] = jnp.zeros_like(o_acc)
    dq_acc[...] = jnp.zeros_like(dq_acc)
    for h in range(heads):
        qt[h] = query[:, h * hs:(h + 1) * hs].T
        ut[h] = jnp.where(valid_t, cot[:, h * hs:(h + 1) * hs].T.astype(F32), 0.0).astype(BF16)

    def rows8(x, op):
        return op(x.reshape(rows // 8, 8, rows), axis=0)

    def scores(b, top):
        key = kv[b, :, :hs]
        i = lax.broadcasted_iota(jnp.int32, (rows, 1), 0)
        j = jnp.where(i < counts[b], b * rows + i, -1)
        allowed = (j >= lo) & (j < hi)
        new = []
        for h in range(heads):
            s = jnp.where(allowed, matmul(key, qt[h]), MASKED)
            s_buf[b, h] = s
            new.append(jnp.maximum(top[h], rows8(s, jnp.max)))
        return tuple(new)

    start = jnp.full((8, rows), MASKED, F32)
    top = lax.fori_loop(b_lo, b_hi, scores, (start,) * heads)
    top = [jnp.max(t, axis=0, keepdims=True) * c for t in top]

    def weigh(b, total_of):
        value_t = kv[b, :, hs:].T
        new = []
        for h in range(heads):
            e = jnp.exp2(s_buf[b, h] * c - top[h])
            new.append(total_of[h] + rows8(e, jnp.sum))
            e = e.astype(BF16)
            e_buf[b, h] = e
            o_acc[h] += matmul(value_t, e)
        return tuple(new)

    totals = lax.fori_loop(b_lo, b_hi, weigh, (jnp.zeros((8, rows), F32),) * heads)
    us, deltas = [], []
    for h in range(heads):
        part = 1.0 / jnp.sum(totals[h], axis=0, keepdims=True)
        attended = jnp.where(valid_t, o_acc[h] * part, 0.0)
        ctx[:, h * hs:(h + 1) * hs] = attended.T.astype(BF16)
        u = ut[h].astype(F32) * part
        deltas.append(jnp.sum(u * attended, axis=0, keepdims=True))
        ut[h] = u.astype(BF16)
        us.append(u.T.astype(BF16))

    def back(b, carry):
        key = kv[b, :, :hs]
        value = kv[b, :, hs:]
        key_t = key.T
        dkey = dval = None
        for h in range(heads):
            e = e_buf[b, h]
            ds = (e.astype(F32) * (matmul(value, ut[h]) - deltas[h])).astype(BF16)
            dq_acc[h] += matmul(key_t, ds)
            k_term = matmul(ds, query[:, h * hs:(h + 1) * hs])
            v_term = matmul(e, us[h])
            dkey = k_term if dkey is None else dkey + k_term
            dval = v_term if dval is None else dval + v_term
        dkv[b, :, :hs] = (dkey * hs ** -0.5).astype(BF16)
        dkv[b, :, hs:] = dval.astype(BF16)
        return carry

    lax.fori_loop(b_lo, b_hi, back, 0)
    for h in range(heads):
        dquery[:, h * hs:(h + 1) * hs] = (dq_acc[h] * hs ** -0.5).T.astype(BF16)


def attention(heads, me, span, counts, seg, query, kv, cot):
    rows, qcols = query.shape
    hs = qcols // heads
    blocks = kv.shape[0]
    vmem = pl.BlockSpec(memory_space=pltpu.VMEM)
    smem = pl.BlockSpec(memory_space=pltpu.SMEM)
    return pl.pallas_call(
        functools.partial(attention_kernel, heads),
        out_shape=[
            jax.ShapeDtypeStruct((rows, qcols), BF16),
            jax.ShapeDtypeStruct((rows, qcols), BF16),
            jax.ShapeDtypeStruct(kv.shape, BF16),
        ],
        in_specs=[smem] * 3 + [vmem] * 4,
        out_specs=[vmem] * 3,
        scratch_shapes=[
            pltpu.VMEM((blocks, heads, rows, rows), F32),
            pltpu.VMEM((blocks, heads, rows, rows), BF16),
            pltpu.VMEM((heads, hs, rows), BF16),
            pltpu.VMEM((heads, hs, rows), BF16),
            pltpu.VMEM((heads, hs, rows), F32),
            pltpu.VMEM((heads, hs, rows), F32),
        ],
        compiler_params=pltpu.CompilerParams(vmem_limit_bytes=48 * MIB),
        name="attention",
    )(me, span, counts, seg, query, kv, cot)


def scatter_kernel(
    sizes, total, dkvp, dq, x2t, wq, wkv, acc_q, acc_kv, gt, out_q, out_kv,
    own, sib, dq2, dkv2, x2, wqb, wkvb, cyc_q, cyc_kv,
    kv_send, kv_recv, fq_send, fq_recv, fk_send, fk_recv, y_send, y_recv, back_q, back_kv, back_q_in, back_kv_in,
    send, recv, local,
):
    place = Place(*sizes)
    links = Links(send, recv)
    chips, half = place.chips, place.chips // 2
    n_tensor = sizes[2]
    rows, qcols = dq.shape
    krows, kcols = wkv.shape[2], wkv.shape[3]
    sub = krows // 2
    c = place.core
    halves = (slice(0, sub), slice(sub, krows))

    loads = []

    def load(src, dst):
        made = pltpu.make_async_copy(src, dst, local.at[len(loads)])
        made.start()
        loads.append(made)
        return made.wait

    have_dq = load(dq, dq2.at[pl.ds(0, rows)])
    have_own = load(dkvp.at[:, c], own)
    have_x = load(x2t, x2)
    have_wq = load(wq, wqb)
    have_wkv = load(wkv, wkvb)
    place.greet()

    distances = [half]
    for d in range(half - 1, 0, -1):
        distances += [d, -d]
    distances.append(0)
    from_sibling = {}
    for d in distances[:1]:
        from_sibling[d] = links.copy(dkvp.at[place.at(d), 1 - c], sib.at[place.at(d)], place.sibling)
    sib_dq = links.copy(dq, dq2.at[pl.ds(rows, rows)], place.sibling)
    for d in distances[1:]:
        from_sibling[d] = links.copy(dkvp.at[place.at(d), 1 - c], sib.at[place.at(d)], place.sibling)
    from_sibling[-half] = lambda: None
    got_cyc_q = links.copy(acc_q, cyc_q, place.along_blk(1))
    got_cyc_kv = links.copy(acc_kv, cyc_kv, place.along_blk(1))

    class Ring:
        def __init__(self, term, sign, n, out, came, first=None):
            self.term, self.sign, self.n, self.out, self.came = term, sign, n, out, came
            self.first, self.k, self.wait = first, 0, None

        def part(self, k):
            return self.first if k == 1 and self.first is not None else slice(0, self.out.shape[1])

        def ref(self, buf, k):
            part = self.part(k)
            return buf.at[k - 1, pl.ds(part.start, part.stop - part.start)]

        def step(self):
            if self.k == self.n:
                return
            self.k = k = self.k + 1
            part = self.part(k)
            value = self.term(self.sign * (self.n - k + 1), part)
            if k == 1:
                self.out[0, part] = value.astype(BF16)
            else:
                before = self.part(k - 1)
                self.wait()
                came = self.came[k - 2, before].astype(F32)
                if before == part:
                    self.out[k - 1] = (value + came).astype(BF16)
                else:
                    other = halves[1] if before == halves[0] else halves[0]
                    self.out[k - 1, before] = (value[before] + came).astype(BF16)
                    self.out[k - 1, other] = value[other].astype(BF16)
            self.wait = links.copy(
                self.ref(self.out, k), self.ref(self.came, k), place.along_seq(self.sign)
            )

        def result(self):
            self.wait()
            return self.came[self.n - 1].astype(F32)

    def kv_term(d, part):
        if part.start == 0 or d != half and d != -half:
            from_sibling[d]()
        here = place.at(d)
        return own[here, part].astype(F32) + sib[here, part].astype(F32)

    def q_term(offset):
        return lambda d, part: matmul(x2[place.at(d), offset:offset + sub], dq2[...])

    def k_term(d, part):
        return matmul(x2[place.at(d), part], dkv2[...])

    kv_rings = [
        Ring(kv_term, sign, half, kv_send.at[i], kv_recv.at[i], halves[i]) for i, sign in enumerate((1, -1))
    ]
    q_rings = []
    for h in range(2):
        for i, sign in enumerate((1, -1)):
            n = half if h == i else half - 1
            q_rings.append(
                Ring(q_term(h * sub), sign, n, fq_send.at[2 * h + i], fq_recv.at[2 * h + i])
            )
    k_rings = [
        Ring(k_term, sign, half, fk_send.at[i], fk_recv.at[i], halves[i]) for i, sign in enumerate((1, -1))
    ]

    def step(rings):
        for ring in rings:
            ring.step()

    long_q = [q_rings[0], q_rings[3]]
    short_q = [q_rings[2], q_rings[1]]

    have_own()
    step(kv_rings)
    have_dq()
    have_x()
    sib_dq()
    step(long_q)
    step(kv_rings)
    step(short_q)
    step(kv_rings)
    step(long_q)
    step(kv_rings)
    step(short_q)
    from_sibling[0]()
    dkeyval = own[place.chip].astype(F32) + sib[place.chip].astype(F32)
    step(long_q)
    dkeyval += kv_rings[0].result() + kv_rings[1].result()
    dkv2[:rows] = dkeyval.astype(BF16)
    sib_dkv = links.copy(dkv2.at[pl.ds(0, rows)], dkv2.at[pl.ds(rows, rows)], place.sibling)

    have_wq()
    have_wkv()
    per = chips // n_tensor

    def grad_term(distance, part):
        t = place.tensor_at(distance)
        shard = 2 * per * krows
        w_q = wqb[pl.ds(t * per, per)].reshape(shard, qcols)
        w_kv = wkvb[pl.ds(t * per, per)].reshape(shard, kcols)
        return matmul_t(dq2[part], w_q) + matmul_t(dkv2[part], w_kv)

    rsub = rows // 2
    rhalves = (slice(0, rsub), slice(rsub, rows))
    y_far = []
    far = grad_term(2, slice(0, rows))
    for i, sign in enumerate((1, -1)):
        y_send[i, 0, rhalves[i]] = far[rhalves[i]].astype(BF16)
        ref = pl.ds(rhalves[i].start, rsub)
        y_far.append(links.copy(y_send.at[i, 0, ref], y_recv.at[i, 0, ref], place.along_tensor(sign)))
    sib_dkv()
    step(k_rings)
    step(short_q)
    step(k_rings)
    y_near = []
    for i, sign in enumerate((1, -1)):
        near = grad_term(sign, slice(0, rows))
        y_far[i]()
        mine, other = rhalves[i], rhalves[1 - i]
        y_send[i, 1, mine] = (near[mine] + y_recv[i, 0, mine].astype(F32)).astype(BF16)
        y_send[i, 1, other] = near[other].astype(BF16)
        y_near.append(links.copy(y_send.at[i, 1], y_recv.at[i, 1], place.along_tensor(sign)))
    step(long_q)
    step(k_rings)
    fresh = []
    for h in range(2):
        mine = matmul(x2[place.chip, halves[h]], dq2[...])
        fresh.append(mine + q_rings[2 * h].result() + q_rings[2 * h + 1].result())
    step(k_rings)
    got_back_q = []
    for h in range(2):
        back_q[halves[h]] = (fresh[h] / total).astype(BF16)
        ref = pl.ds(halves[h].start, sub)
        got_back_q.append(links.copy(back_q.at[ref], back_q_in.at[ref], place.along_blk(-1)))
    home = grad_term(0, slice(0, rows))
    for wait in y_near:
        wait()
    gt[...] = (home + y_recv[0, 1].astype(F32) + y_recv[1, 1].astype(F32)).astype(BF16)
    fresh_kv = matmul(x2[place.chip], dkv2[...]) + k_rings[0].result() + k_rings[1].result()
    back_kv[...] = (fresh_kv / total).astype(BF16)
    got_back_kv = links.copy(back_kv, back_kv_in, place.along_blk(-1))
    got_cyc_q()
    got_cyc_kv()
    for got in got_back_q:
        got()
    out_q[...] = cyc_q[...] + back_q_in[...].astype(F32)
    got_back_kv()
    out_kv[...] = cyc_kv[...] + back_kv_in[...].astype(F32)
    links.drain()


def scatter_grads(sizes, total, dkvp, dq, x2t, wq, wkv, acc_q, acc_kv, width):
    n_blk, n_seq, n_tensor = sizes
    chips = n_seq // 2
    half = chips // 2
    rows, qcols = dq.shape
    krows, kcols = wkv.shape[2], wkv.shape[3]
    sub = krows // 2
    hbm = pl.BlockSpec(memory_space=pl.ANY)
    vmem = pl.BlockSpec(memory_space=pltpu.VMEM)
    return pl.pallas_call(
        functools.partial(scatter_kernel, sizes, total),
        out_shape=[
            jax.ShapeDtypeStruct((rows, width), BF16),
            jax.ShapeDtypeStruct((krows, qcols), F32),
            jax.ShapeDtypeStruct((krows, kcols), F32),
        ],
        in_specs=[hbm] * 7,
        out_specs=[vmem] * 3,
        scratch_shapes=[
            pltpu.VMEM((chips, rows, kcols), BF16),
            pltpu.VMEM((chips, rows, kcols), BF16),
            pltpu.VMEM((2 * rows, qcols), BF16),
            pltpu.VMEM((2 * rows, kcols), BF16),
            pltpu.VMEM(x2t.shape, BF16),
            pltpu.VMEM(wq.shape, BF16),
            pltpu.VMEM(wkv.shape, BF16),
            pltpu.VMEM((krows, qcols), F32),
            pltpu.VMEM((krows, kcols), F32),
            pltpu.VMEM((2, half, rows, kcols), BF16),
            pltpu.VMEM((2, half, rows, kcols), BF16),
            pltpu.VMEM((4, half, sub, qcols), BF16),
            pltpu.VMEM((4, half, sub, qcols), BF16),
            pltpu.VMEM((2, half, krows, kcols), BF16),
            pltpu.VMEM((2, half, krows, kcols), BF16),
            pltpu.VMEM((2, 2, rows, width), BF16),
            pltpu.VMEM((2, 2, rows, width), BF16),
            pltpu.VMEM((krows, qcols), BF16),
            pltpu.VMEM((krows, kcols), BF16),
            pltpu.VMEM((krows, qcols), BF16),
            pltpu.VMEM((krows, kcols), BF16),
            pltpu.SemaphoreType.DMA((64,)),
            pltpu.SemaphoreType.DMA((64,)),
            pltpu.SemaphoreType.DMA((5,)),
        ],
        compiler_params=pltpu.CompilerParams(
            collective_id=1, has_side_effects=True, vmem_limit_bytes=56 * MIB
        ),
        name="scatter_grads",
    )(dkvp, dq, x2t, wq, wkv, acc_q, acc_kv)


def on_device(
    sizes, tokens, w_query, w_keyval, accum_query, accum_keyval, cotangent, seg_ids, spans, counts
):
    n_seq = sizes[1]
    rows, width = tokens.shape[1:]
    krows, qcols = w_query.shape[1:]
    groups, kv_cols = w_keyval.shape[2:]
    kcols = groups * kv_cols
    heads = qcols // (kv_cols // 2)
    total = rows * n_seq
    x2t, wq_all, wkv_all, kv_all, query = gather_project(
        sizes, tokens[0], w_query[0], w_keyval[0].reshape(krows, kcols)
    )
    me = lax.axis_index("seq").astype(jnp.int32).reshape(1)
    context, dquery, dkv = attention(
        heads, me, spans[0].reshape(-1), counts[0], seg_ids[0].reshape(n_seq, rows),
        query, kv_all.reshape(n_seq, rows, kcols), cotangent[0],
    )
    grad_tokens, out_q, out_kv = scatter_grads(
        sizes, total, dkv.reshape(kv_all.shape), dquery, x2t, wq_all, wkv_all,
        accum_query[0], accum_keyval[0].reshape(krows, kcols), width,
    )
    return context[None], grad_tokens[None], out_q[None], out_kv.reshape(w_keyval.shape)


def solution(mesh):
    sizes = (mesh.shape["blk"], mesh.shape["seq"], mesh.shape["tensor"])
    in_specs = (
        P("blk", "seq", "tensor"),
        P("blk", "seq", "tensor"),
        P("blk", "seq", "tensor", None),
        P("blk", "seq", "tensor"),
        P("blk", "seq", "tensor", None),
        P("blk", "seq", "tensor"),
        P("blk", None),
        P("blk", None, None),
        P("blk", None),
    )
    out_specs = (
        P("blk", "seq", "tensor"),
        P("blk", "seq", "tensor"),
        P("blk", "seq", "tensor"),
        P("blk", "seq", "tensor", None),
    )
    return jax.shard_map(
        functools.partial(on_device, sizes), mesh=mesh, in_specs=in_specs, out_specs=out_specs, check_vma=False
    )
```

```python
import functools

import jax
import jax.numpy as jnp
from jax import lax
from jax.experimental import pallas as pl
from jax.experimental.pallas import tpu as pltpu
from jax.sharding import PartitionSpec as P

MESH = pl.DeviceIdType.MESH
BF16 = jnp.bfloat16
F32 = jnp.float32
MIB = 1 << 20
LOG2E = 1.4426950408889634
MASKED = -1e30
PAIR = 2
FILLS = (0, 1, 2, 0, 2, 1, 0, 2, 0, 2, 1, 0, 0, 1, 2, 1, 1, 0, 2, 5, 0, 1, 1, 1, 1, 2, 2, 1, 2, 2, 1, 0, 0, 1, 2)


def matmul(a, b):
    return jnp.dot(a, b, preferred_element_type=F32)


def matmul_t(a, b):
    return lax.dot_general(a, b, (((1,), (1,)), ((), ())), preferred_element_type=F32)


class Place:
    def __init__(self, n_blk, n_seq, n_tensor):
        self.n_blk, self.chips, self.n_tensor = n_blk, n_seq // 2, n_tensor
        me = lax.axis_index("seq")
        self.core, self.chip = lax.rem(me, 2), lax.div(me, 2)
        self.blk, self.t = lax.axis_index("blk"), lax.axis_index("tensor")
        self.sibling = {"seq": me + 1 - 2 * self.core}

    def at(self, distance):
        return lax.rem(self.chip + distance + self.chips, self.chips)

    def along_seq(self, distance):
        return {"seq": 2 * self.at(distance) + self.core}

    def along_blk(self, distance):
        return {"blk": lax.rem(self.blk + distance + self.n_blk, self.n_blk)}

    def tensor_at(self, distance):
        return lax.rem(self.t + distance + self.n_tensor, self.n_tensor)

    def along_tensor(self, distance):
        return {"tensor": self.tensor_at(distance)}

    def greet(self):
        barrier = pltpu.get_barrier_semaphore()
        others = [self.sibling]
        for sign in (1, -1):
            others += [self.along_seq(sign), self.along_blk(sign), self.along_tensor(sign)]
        for other in others:
            pl.semaphore_signal(barrier, inc=1, device_id=other, device_id_type=MESH)
        pl.semaphore_wait(barrier, len(others))


class Links:
    def __init__(self, send, recv):
        self.send, self.recv, self.used, self.sent = send, recv, 0, []

    def copy(self, src, dst, to, arrives=None):
        i = self.used
        self.used += 1
        made = pltpu.make_async_remote_copy(
            src_ref=src, dst_ref=dst, send_sem=self.send.at[i], recv_sem=self.recv.at[i],
            device_id=to, device_id_type=MESH,
        )
        landing = made
        if arrives is not None:
            landing = pltpu.make_async_remote_copy(
                src_ref=arrives, dst_ref=arrives, send_sem=self.send.at[i], recv_sem=self.recv.at[i],
                device_id=to, device_id_type=MESH,
            )
        made.start()
        self.sent.append(made)
        return landing.wait_recv

    def drain(self):
        for made in self.sent:
            made.wait_send()


class Gather:
    def __init__(self, place, links, buf):
        self.place, self.links, self.buf = place, links, buf
        self.half = place.chips // 2
        sub = buf.shape[2] // 2
        self.parts = (pl.ds(0, sub), pl.ds(sub, sub))
        self.done, self.waits, self.shares, self.finished = [0, 0], [None, None], [], False

    def start(self, h):
        place, c = self.place, self.place.core
        self.done[h] = step = self.done[h] + 1
        self.waits[h] = []
        for i, sign in enumerate((1, -1)):
            if step == self.half and i != h:
                continue
            src = self.buf.at[place.at(-sign * (step - 1)), c, self.parts[h]]
            lands = self.buf.at[place.at(-sign * step), c, self.parts[h]]
            self.waits[h].append(self.links.copy(src, src, place.along_seq(sign), lands))

    def share(self, distance):
        place = self.place
        src = self.buf.at[place.at(distance), place.core]
        lands = self.buf.at[place.at(distance), 1 - place.core]
        self.shares.append(self.links.copy(src, src, place.sibling, lands))

    def advance(self, h):
        step = self.done[h]
        for wait in self.waits[h]:
            wait()
        if step < self.half:
            self.start(h)
        if h == 1:
            self.finished = step == self.half
            for distance in (step, -step) if step < self.half else (step,):
                self.share(distance)

    def collect(self):
        for wait in self.shares:
            wait()


class Scatter:
    def __init__(self, place, links, term, out, came):
        self.place, self.links, self.term, self.out, self.came = place, links, term, out, came
        self.half = place.chips // 2
        self.sub = out.shape[2]
        self.done, self.waits = [0, 0], [[None, None], [None, None]]

    def rows(self, h):
        return slice(h * self.sub, (h + 1) * self.sub)

    def reach(self, h, i):
        return self.half if h == i else self.half - 1

    def step(self, h):
        self.done[h] = k = self.done[h] + 1
        for i, sign in enumerate((1, -1)):
            n = self.reach(h, i)
            if k > n:
                continue
            at = 2 * h + i
            value = self.term(sign * (n - k + 1), self.rows(h))
            if k > 1:
                self.waits[h][i]()
                value += self.came[at, k - 2].astype(F32)
            self.out[at, k - 1] = value.astype(BF16)
            self.waits[h][i] = self.links.copy(
                self.out.at[at, k - 1], self.came.at[at, k - 1], self.place.along_seq(sign)
            )

    def result(self, h):
        value = self.term(0, self.rows(h))
        for i in range(2):
            self.waits[h][i]()
            value += self.came[2 * h + i, self.reach(h, i) - 1].astype(F32)
        return value


def layer_kernel(
    sizes, heads, pair, total, tok, wq, wkv, cot, acc_q, acc_kv, seg, span, counts,
    ctx_out, gt_out, out_q_out, out_kv_out,
    ctx, gt, out_q, out_kv, xb, x2t, xts, wqbs, wkvb, kvb, cotb, qb, qt, ut, bias, s_buf, e_buf, o_acc, dq_acc, dk_acc, dkvb, sib,
    dq2, dkv2, rq_send, rq_recv, r_send, r_recv, y_send, y_recv, back_q, back_q_in, back_kv, back_kv_in,
    cyc_q, cyc_kv, send, recv, local,
):
    place = Place(*sizes)
    links = Links(send, recv)
    n_tensor = sizes[2]
    chips, half = place.chips, place.chips // 2
    per = chips // n_tensor
    rows = tok.shape[0]
    krows, kcols = wkv.shape
    hs = kcols // 2
    groups = heads // pair
    pcols = pair * hs
    c = place.core
    sub, rsub = krows // 2, rows // 2
    wqb = [wqbs.at[g] for g in range(groups)]

    own_tok = pltpu.make_async_copy(tok, xb.at[place.t], local.at[0])
    own_tok.start()
    own_cot = pltpu.make_async_copy(cot, cotb, local.at[1])
    own_cot.start()
    place.greet()

    ahead = place.along_blk(1)
    halves = (pl.ds(0, sub), pl.ds(sub, sub))
    shift_kv = [links.copy(wkv.at[h], wkvb.at[place.chip, c, h], ahead) for h in halves]
    rhalves = (pl.ds(0, rsub), pl.ds(rsub, rsub))
    near = [[None, None], [None, None]]
    for first in range(2):
        for i, sign in enumerate((1, -1)):
            h = i if first == 0 else 1 - i
            near[i][h] = links.copy(
                tok.at[rhalves[h]], xb.at[place.t, rhalves[h]], place.along_tensor(sign),
                xb.at[place.tensor_at(-sign), rhalves[h]],
            )
    shift_q = [
        links.copy(wq.at[:, pl.ds(p * pcols, pcols)], wqb[p].at[place.chip, c], ahead)
        for p in range(groups)
    ]

    g_wkv = Gather(place, links, wkvb)
    g_wq = [Gather(place, links, buf) for buf in wqb]
    g_kv = Gather(place, links, kvb)

    later = []

    counts_of = iter(FILLS)

    def fill(n=None):
        for _ in range(next(counts_of) if n is None else n):
            if later:
                later.pop(0)()

    def both(ring, move="advance"):
        for h in range(2):
            getattr(ring, move)(h)

    def first_share(p):
        shift_q[p]()
        g_wq[p].share(0)
        g_wq[p].start(0)

    for p in range(groups):
        later.append(functools.partial(first_share, p))
        later.append(functools.partial(g_wq[p].start, 1))
        for _ in range(half):
            later.append(functools.partial(g_wq[p].advance, 0))
            later.append(functools.partial(g_wq[p].advance, 1))

    for h in range(2):
        shift_kv[h]()
        g_wkv.start(h)
    g_wkv.share(0)
    both(g_wkv)
    fill()
    far = []
    for i, sign in enumerate((1, -1)):
        near[i][i]()
        src = xb.at[place.tensor_at(-sign), rhalves[i]]
        far.append(links.copy(
            src, src, place.along_tensor(sign), xb.at[place.tensor_at(-2 * sign), rhalves[i]]
        ))
    fill()

    me = 2 * place.chip + c
    slots = span.shape[1]
    seg_all = seg[...]
    seg_q = seg[:, pl.ds(pl.multiple_of(me * rows, rows), rows)]
    lane = lax.broadcasted_iota(jnp.int32, (1, rows), 1)
    qpos = me * rows + lane
    lo = jnp.zeros((1, rows), jnp.int32)
    hi = jnp.zeros((1, rows), jnp.int32)
    begin = jnp.zeros((1, 1), jnp.int32)
    for s in range(slots):
        end = jnp.sum((seg_all <= s).astype(F32), axis=1, keepdims=True).astype(jnp.int32)
        first, last = span[0, s, 0], span[0, s, 1]
        here = seg_q == s
        inside = (qpos >= first) & (qpos < last)
        lo = jnp.where(here, begin, lo)
        hi = jnp.where(here, jnp.where(inside, jnp.minimum(last, end), qpos + 1), hi)
        begin = end
    valid_t = lane < counts[0, me]
    row = lax.broadcasted_iota(jnp.int32, (rows, 1), 0)

    def mask(blocks):
        for b in blocks:
            j = jnp.where(row < counts[0, b], b * rows + row, -1)
            bias[b] = jnp.where((j >= lo) & (j < hi), 0.0, MASKED)

    mask(range(chips))
    both(g_wkv)
    fill()
    mask(range(chips, 2 * chips))
    both(g_wkv)
    fill()
    own_cot.wait()
    for h in range(heads):
        u = cotb[:, h * hs:(h + 1) * hs].T
        ut[h] = jnp.where(valid_t, u.astype(F32), 0.0).astype(BF16)
    fill()
    both(g_wkv)
    fill()
    for i in range(2):
        near[i][1 - i]()
        far[i]()
    own_tok.wait()
    g_wkv.collect()

    def project(buf):
        out = None
        for t in range(n_tensor):
            part = buf[t * per:(t + 1) * per].reshape(2 * per * krows, buf.shape[3])
            term = matmul(xb[t], part)
            out = term if out is None else out + term
        return out.astype(BF16)

    kvb[place.chip, c] = project(wkvb)
    both(g_kv, "start")
    g_kv.share(0)
    fill()
    saves = []

    def save(src, dst):
        saves.append(pltpu.make_async_copy(src, dst, local.at[2 + len(saves)]))
        saves[-1].start()

    got_cyc = [links.copy(acc_q, cyc_q, ahead), links.copy(acc_kv, cyc_kv, ahead)]

    x_got = []

    def turn(t):
        for p in range(per):
            z = t * per + p
            mine = pl.ds(pl.multiple_of((2 * p + c) * krows, krows), krows)
            other = pl.ds(pl.multiple_of((2 * p + 1 - c) * krows, krows), krows)
            x2t[z, :, :rows] = xb[t, :, mine].T
            xts[z] = xb[t, :, other].T
        z = pl.ds(t * per, per)
        x_got.append(links.copy(xts.at[z], x2t.at[z, :, pl.ds(rows, rows)], place.sibling))

    def queries(p):
        while not g_wq[p].finished:
            fill(1)
        g_wq[p].collect()
        qb[p] = project(wqb[p])
        for i in range(pair):
            qt[pair * p + i] = qb[p, :, i * hs:(i + 1) * hs].T

    turns = list(range(n_tensor))
    for step in range(half):
        for _ in range(2 if step == 1 else 1):
            if turns:
                turn(turns.pop(0))
        if step == half - 1:
            queries(0)
        fill()
        both(g_kv)
        fill()
    while turns:
        turn(turns.pop(0))
    g_kv.collect()

    def rows8(x, op):
        return op(x.reshape(x.shape[0] // 8, 8, rows), axis=0)

    scale = hs ** -0.5
    n_keys = chips * rows

    def attend(p):
        last = p == groups - 1

        def tick(enough=False):
            if not enough:
                fill()

        tops = [jnp.full((8, rows), MASKED, F32)] * pair
        for part in range(2):
            z = slice(part * half, (part + 1) * half)
            b = slice(part * chips, (part + 1) * chips)
            for i in range(pair):
                key = kvb[z, :, :, :hs].reshape(n_keys, hs)
                s = matmul(key, qt[pair * p + i]) + bias[b].reshape(n_keys, rows)
                s_buf[i, part] = s
                tops[i] = jnp.maximum(tops[i], rows8(s, jnp.max))
            tick()
        tops = [jnp.max(t, axis=0, keepdims=True) * (scale * LOG2E) for t in tops]
        sums = [jnp.zeros((8, rows), F32)] * pair
        for part in range(2):
            z = slice(part * half, (part + 1) * half)
            for i in range(pair):
                e = jnp.exp2(s_buf[i, part] * (scale * LOG2E) - tops[i])
                sums[i] = sums[i] + rows8(e, jnp.sum)
                e = e.astype(BF16)
                e_buf[i, part] = e
                term = matmul(kvb[z, :, :, hs:].reshape(n_keys, hs).T, e)
                o_acc[i] = term if part == 0 else o_acc[i] + term
            tick()
        us, deltas = [], []
        for i in range(pair):
            h = pair * p + i
            inverse = 1.0 / jnp.sum(sums[i], axis=0, keepdims=True)
            attended = jnp.where(valid_t, o_acc[i] * inverse, 0.0)
            ctx[:, h * hs:(h + 1) * hs] = attended.T.astype(BF16)
            u = ut[h].astype(F32) * inverse
            deltas.append(jnp.sum(u * attended, axis=0, keepdims=True))
            ut[h] = u.astype(BF16)
            us.append(u.T.astype(BF16))
        for part in range(2):
            z = slice(part * half, (part + 1) * half)
            dkey = dval = None
            for i in range(pair):
                h = pair * p + i
                e = e_buf[i, part]
                dp = matmul(kvb[z, :, :, hs:].reshape(n_keys, hs), ut[h])
                ds = (e.astype(F32) * (dp - deltas[i])).astype(BF16)
                term = matmul(kvb[z, :, :, :hs].reshape(n_keys, hs).T, ds)
                dq_acc[i] = term if part == 0 else dq_acc[i] + term
                k_term = matmul(ds, qb[p, :, i * hs:(i + 1) * hs])
                v_term = matmul(e, us[i])
                dkey = k_term if dkey is None else dkey + k_term
                dval = v_term if dval is None else dval + v_term
            if p > 0:
                dkey += dk_acc[part, :, :hs]
                dval += dk_acc[part, :, hs:]
            if last:
                dkvb[z, :, :, :hs] = (dkey * scale).astype(BF16).reshape(half, 2, rows, hs)
                dkvb[z, :, :, hs:] = dval.astype(BF16).reshape(half, 2, rows, hs)
                zz = pl.ds(part * half, half)
                exchanged.append(links.copy(dkvb.at[zz, 1 - c], sib.at[zz], place.sibling))
            else:
                dk_acc[part, :, :hs] = dkey
                dk_acc[part, :, hs:] = dval
            tick(part == 1)
        for i in range(pair):
            dq2[p, :rows, i * hs:(i + 1) * hs] = (dq_acc[i] * scale).T.astype(BF16)
        mine = dq2.at[p, pl.ds(0, rows)]
        got_dq = links.copy(mine, dq2.at[p, pl.ds(rows, rows)], place.sibling)

        def first_step():
            got_dq()
            s_q[p].step(0)

        later.append(first_step)
        later.append(functools.partial(s_q[p].step, 1))
        for _ in range(half - 1):
            later.append(functools.partial(s_q[p].step, 0))
            later.append(functools.partial(s_q[p].step, 1))
        later.append(functools.partial(hand_back, s_q[p], back_q.at[p], back_q_in.at[p], 0))
        later.append(functools.partial(hand_back, s_q[p], back_q.at[p], back_q_in.at[p], 1))

    exchanged = []

    def fresh_term(grads):
        return lambda d, part: matmul(x2t[place.at(d), part], grads[...])

    def kv_term(d, part):
        here = place.at(d)
        return dkvb[here, c, part].astype(F32) + sib[here, part].astype(F32)

    s_q = [
        Scatter(place, links, fresh_term(dq2.at[p]), rq_send.at[p], rq_recv.at[p]) for p in range(groups)
    ]
    s_kv = Scatter(place, links, kv_term, r_send.at[0], r_recv.at[0])
    s_k = Scatter(place, links, fresh_term(dkv2), r_send.at[1], r_recv.at[1])
    got_back = []

    def hand_back(scatter, out, came, h):
        part = pl.ds(h * sub, sub)
        out[part] = (scatter.result(h) / total).astype(BF16)
        got_back.append(links.copy(out.at[part], came.at[part], place.along_blk(-1)))

    attend(0)
    for wait in x_got:
        wait()
    for p in range(1, groups):
        queries(p)
        fill()
        attend(p)
    save(ctx, ctx_out)
    for wait in exchanged:
        wait()
    for _ in range(half):
        both(s_kv, "step")
        fill()
    for h in range(2):
        dkv2[h * rsub:(h + 1) * rsub] = s_kv.result(h).astype(BF16)
    got_dkv = links.copy(dkv2.at[pl.ds(0, rows)], dkv2.at[pl.ds(rows, rows)], place.sibling)

    shard = 2 * per * krows

    def grad_term(distance, part):
        t = place.tensor_at(distance)
        value = matmul_t(dkv2[part], wkvb[pl.ds(t * per, per)].reshape(shard, kcols))
        for p in range(groups):
            value += matmul_t(dq2[p, part], wqb[p][pl.ds(t * per, per)].reshape(shard, pcols))
        return value

    def row_half(h):
        return slice(h * rsub, (h + 1) * rsub)

    y_far, y_near = [], [[None, None], [None, None]]
    for i, sign in enumerate((1, -1)):
        y_send[i, 0] = grad_term(2, row_half(i)).astype(BF16)
        y_far.append(links.copy(y_send.at[i, 0], y_recv.at[i, 0], place.along_tensor(sign)))
    got_dkv()
    both(s_k, "step")
    for i, sign in enumerate((1, -1)):
        y_send[i, 1] = grad_term(sign, row_half(1 - i)).astype(BF16)
        y_near[i][1 - i] = links.copy(y_send.at[i, 1], y_recv.at[i, 1], place.along_tensor(sign))
    fill()
    both(s_k, "step")
    fill()
    for i, sign in enumerate((1, -1)):
        value = grad_term(sign, row_half(i))
        y_far[i]()
        y_send[i, 2] = (value + y_recv[i, 0].astype(F32)).astype(BF16)
        y_near[i][i] = links.copy(y_send.at[i, 2], y_recv.at[i, 2], place.along_tensor(sign))
    fill()
    for _ in range(half - 2):
        both(s_k, "step")
        fill()
    home = [grad_term(0, row_half(h)) for h in range(2)]
    for h in range(2):
        hand_back(s_k, back_kv, back_kv_in, h)
    fill(len(later))
    for h in range(2):
        value = home[h]
        for i in range(2):
            y_near[i][h]()
            value += y_recv[i, 2 if h == i else 1].astype(F32)
        gt[row_half(h)] = value.astype(BF16)
    save(gt, gt_out)
    for wait in got_cyc:
        wait()
    for got in got_back:
        got()
    for i in range(2):
        cols = slice(i * hs, (i + 1) * hs)
        out_kv[:, i, :] = cyc_kv[:, i, :] + back_kv_in[:, cols].astype(F32)
    save(out_kv, out_kv_out)
    for p in range(groups):
        cols = slice(p * pcols, (p + 1) * pcols)
        out_q[:, cols] = cyc_q[:, cols] + back_q_in[p].astype(F32)
    save(out_q, out_q_out)
    links.drain()
    for made in saves:
        made.wait()


def layer(sizes, heads, pair, tok, wq, wkv, cot, acc_q, acc_kv, seg, span, counts):
    n_blk, n_seq, n_tensor = sizes
    chips = n_seq // 2
    half = chips // 2
    rows, width = tok.shape
    krows, qcols = wq.shape
    kcols = wkv.shape[1]
    hs = kcols // 2
    groups = heads // pair
    pcols = pair * hs
    n_keys = chips * rows
    sub, rsub = krows // 2, rows // 2
    hbm = pl.BlockSpec(memory_space=pl.ANY)
    vmem = pl.BlockSpec(memory_space=pltpu.VMEM)
    smem = pl.BlockSpec(memory_space=pltpu.SMEM)

    def weights(cols):
        return pltpu.VMEM((chips, 2, krows, cols), BF16)

    outs = [
        jax.ShapeDtypeStruct((rows, qcols), BF16),
        jax.ShapeDtypeStruct((rows, width), BF16),
        jax.ShapeDtypeStruct((krows, qcols), F32),
        jax.ShapeDtypeStruct((krows, 2, hs), F32),
    ]
    scratch = [pltpu.VMEM(out.shape, out.dtype) for out in outs] + [
        pltpu.VMEM((n_tensor, rows, width), BF16),
        pltpu.VMEM((chips, krows, 2 * rows), BF16),
        pltpu.VMEM((chips, krows, rows), BF16),
        pltpu.VMEM((groups, chips, 2, krows, pcols), BF16),
        weights(kcols),
        pltpu.VMEM((chips, 2, rows, kcols), BF16),
        pltpu.VMEM((rows, qcols), BF16),
        pltpu.VMEM((groups, rows, pcols), BF16),
        pltpu.VMEM((heads, hs, rows), BF16),
        pltpu.VMEM((heads, hs, rows), BF16),
        pltpu.VMEM((n_seq, rows, rows), F32),
        pltpu.VMEM((pair, 2, n_keys, rows), F32),
        pltpu.VMEM((pair, 2, n_keys, rows), BF16),
        pltpu.VMEM((pair, hs, rows), F32),
        pltpu.VMEM((pair, hs, rows), F32),
        pltpu.VMEM((2, n_keys, kcols), F32),
        pltpu.VMEM((chips, 2, rows, kcols), BF16),
        pltpu.VMEM((chips, rows, kcols), BF16),
        pltpu.VMEM((groups, 2 * rows, pcols), BF16),
        pltpu.VMEM((2 * rows, kcols), BF16),
        pltpu.VMEM((groups, 4, half, sub, pcols), BF16),
        pltpu.VMEM((groups, 4, half, sub, pcols), BF16),
        pltpu.VMEM((2, 4, half, sub, kcols), BF16),
        pltpu.VMEM((2, 4, half, sub, kcols), BF16),
        pltpu.VMEM((2, 3, rsub, width), BF16),
        pltpu.VMEM((2, 3, rsub, width), BF16),
        pltpu.VMEM((groups, krows, pcols), BF16),
        pltpu.VMEM((groups, krows, pcols), BF16),
        pltpu.VMEM((krows, kcols), BF16),
        pltpu.VMEM((krows, kcols), BF16),
        pltpu.VMEM((krows, qcols), F32),
        pltpu.VMEM((krows, 2, hs), F32),
        pltpu.SemaphoreType.DMA((256,)),
        pltpu.SemaphoreType.DMA((256,)),
        pltpu.SemaphoreType.DMA((6,)),
    ]
    return pl.pallas_call(
        functools.partial(layer_kernel, sizes, heads, pair, rows * n_seq),
        out_shape=outs,
        in_specs=[hbm] * 6 + [vmem, smem, smem],
        out_specs=[hbm] * 4,
        scratch_shapes=scratch,
        compiler_params=pltpu.CompilerParams(
            collective_id=0, has_side_effects=True, vmem_limit_bytes=62 * MIB
        ),
        name="layer",
    )(tok, wq, wkv, cot, acc_q, acc_kv, seg, span, counts)


def hand_over_kernel(count, *refs):
    sems = refs[-1]
    moves = [pltpu.make_async_copy(refs[i], refs[count + i], sems.at[i]) for i in range(count)]
    for move in moves:
        move.start()
    for move in moves:
        move.wait()


def hand_over(*arrays):
    count = len(arrays)
    hbm = pl.BlockSpec(memory_space=pl.ANY)
    return pl.pallas_call(
        functools.partial(hand_over_kernel, count),
        out_shape=[jax.ShapeDtypeStruct(a.shape, a.dtype) for a in arrays],
        in_specs=[pl.BlockSpec(memory_space=pltpu.VMEM)] * count,
        out_specs=[hbm] * count,
        scratch_shapes=[pltpu.SemaphoreType.DMA((count,))],
        compiler_params=pltpu.CompilerParams(vmem_limit_bytes=60 * MIB),
        name="hand_over",
    )(*arrays)


def on_device(
    sizes, tokens, w_query, w_keyval, accum_query, accum_keyval, cotangent, seg_ids, spans, counts
):
    krows, qcols = w_query.shape[1:]
    groups, kv_cols = w_keyval.shape[2:]
    kcols = groups * kv_cols
    context, grad_tokens, out_q, out_kv = layer(
        sizes, qcols // (kv_cols // 2), PAIR, tokens[0], w_query[0], w_keyval[0].reshape(krows, kcols),
        cotangent[0], accum_query[0], accum_keyval[0].reshape(krows, 2, kcols // 2), seg_ids, spans, counts,
    )
    context, grad_tokens, out_q, out_kv = hand_over(context, grad_tokens, out_q, out_kv)
    return context[None], grad_tokens[None], out_q[None], out_kv.reshape(w_keyval.shape)


def solution(mesh):
    sizes = (mesh.shape["blk"], mesh.shape["seq"], mesh.shape["tensor"])
    in_specs = (
        P("blk", "seq", "tensor"),
        P("blk", "seq", "tensor"),
        P("blk", "seq", "tensor", None),
        P("blk", "seq", "tensor"),
        P("blk", "seq", "tensor", None),
        P("blk", "seq", "tensor"),
        P("blk", None),
        P("blk", None, None),
        P("blk", None),
    )
    out_specs = (
        P("blk", "seq", "tensor"),
        P("blk", "seq", "tensor"),
        P("blk", "seq", "tensor"),
        P("blk", "seq", "tensor", None),
    )
    return jax.shard_map(
        functools.partial(on_device, sizes), mesh=mesh, in_specs=in_specs, out_specs=out_specs, check_vma=False
    )
```

```python
import functools

import jax
import jax.numpy as jnp
from jax import lax
from jax.experimental import pallas as pl
from jax.experimental.pallas import tpu as pltpu
from jax.sharding import PartitionSpec as P

MESH = pl.DeviceIdType.MESH
BF16 = jnp.bfloat16
F32 = jnp.float32
MIB = 1 << 20
LOG2E = 1.4426950408889634
MASKED = -1e30
PAIR = 2
FILLS = (0, 1, 2, 0, 2, 1, 0, 2, 1, 2, 1, 0, 1, 0, 2, 0, 1, 1, 1, 2, 0, 1, 1, 1, 1, 2, 2, 2, 1, 2, 1, 0, 0, 1, 2)


def matmul(a, b):
    return jnp.dot(a, b, preferred_element_type=F32)


def matmul_t(a, b):
    return lax.dot_general(a, b, (((1,), (1,)), ((), ())), preferred_element_type=F32)


class Place:
    def __init__(self, n_blk, n_seq, n_tensor):
        self.n_blk, self.chips, self.n_tensor = n_blk, n_seq // 2, n_tensor
        me = lax.axis_index("seq")
        self.core, self.chip = lax.rem(me, 2), lax.div(me, 2)
        self.blk, self.t = lax.axis_index("blk"), lax.axis_index("tensor")
        self.sibling = {"seq": me + 1 - 2 * self.core}

    def at(self, distance):
        return lax.rem(self.chip + distance + self.chips, self.chips)

    def slot(self, distance):
        return (distance - self.chips // 4) % self.chips

    def along_seq(self, distance):
        return {"seq": 2 * self.at(distance) + self.core}

    def along_blk(self, distance):
        return {"blk": lax.rem(self.blk + distance + self.n_blk, self.n_blk)}

    def tensor_at(self, distance):
        return lax.rem(self.t + distance + self.n_tensor, self.n_tensor)

    def along_tensor(self, distance):
        return {"tensor": self.tensor_at(distance)}

    def greet(self):
        barrier = pltpu.get_barrier_semaphore()
        others = [self.sibling]
        for sign in (1, -1):
            others += [self.along_seq(sign), self.along_blk(sign), self.along_tensor(sign)]
        for other in others:
            pl.semaphore_signal(barrier, inc=1, device_id=other, device_id_type=MESH)
        return lambda: pl.semaphore_wait(barrier, len(others))


class Links:
    def __init__(self, send, recv):
        self.send, self.recv, self.used, self.sent = send, recv, 0, []

    def copy(self, src, dst, to, arrives=None):
        i = self.used
        self.used += 1
        made = pltpu.make_async_remote_copy(
            src_ref=src, dst_ref=dst, send_sem=self.send.at[i], recv_sem=self.recv.at[i],
            device_id=to, device_id_type=MESH,
        )
        landing = made
        if arrives is not None:
            landing = pltpu.make_async_remote_copy(
                src_ref=arrives, dst_ref=arrives, send_sem=self.send.at[i], recv_sem=self.recv.at[i],
                device_id=to, device_id_type=MESH,
            )
        made.start()
        self.sent.append(made)
        return landing.wait_recv

    def drain(self):
        for made in self.sent:
            made.wait_send()


class Gather:
    def __init__(self, place, links, buf, by_distance=False):
        self.place, self.links, self.buf = place, links, buf
        self.by_distance = by_distance
        self.slot = place.slot if by_distance else place.at
        self.half = place.chips // 2
        sub = buf.shape[2] // 2
        self.parts = (pl.ds(0, sub), pl.ds(sub, sub))
        self.done, self.waits, self.shares, self.finished, self.taken = [0, 0], [None, None], [], False, 0

    def start(self, h):
        place, c = self.place, self.place.core
        self.done[h] = step = self.done[h] + 1
        self.waits[h] = []
        for i, sign in enumerate((1, -1)):
            if step == self.half and i != h:
                continue
            src = self.buf.at[self.slot(-sign * (step - 1)), c, self.parts[h]]
            lands = self.buf.at[self.slot(-sign * step), c, self.parts[h]]
            there = lands if self.by_distance else src
            self.waits[h].append(self.links.copy(src, there, place.along_seq(sign), lands))

    def share(self, distance):
        place = self.place
        src = self.buf.at[self.slot(distance), place.core]
        lands = self.buf.at[self.slot(distance), 1 - place.core]
        self.shares.append(self.links.copy(src, src, place.sibling, lands))

    def advance(self, h):
        step = self.done[h]
        for wait in self.waits[h]:
            wait()
        if step < self.half:
            self.start(h)
        if h == 1:
            self.finished = step == self.half
            for distance in (step, -step) if step < self.half else (step,):
                self.share(distance)

    def collect(self, count=None):
        shares = self.shares[self.taken:count]
        self.taken += len(shares)
        for wait in shares:
            wait()


class Scatter:
    def __init__(self, place, links, term, out, came):
        self.place, self.links, self.term, self.out, self.came = place, links, term, out, came
        self.half = place.chips // 2
        self.sub = out.shape[2]
        self.done, self.waits = [0, 0], [[None, None], [None, None]]

    def rows(self, h):
        return slice(h * self.sub, (h + 1) * self.sub)

    def reach(self, h, i):
        return self.half if h == i else self.half - 1

    def step(self, h):
        self.done[h] = k = self.done[h] + 1
        for i, sign in enumerate((1, -1)):
            n = self.reach(h, i)
            if k > n:
                continue
            at = 2 * h + i
            value = self.term(sign * (n - k + 1), self.rows(h))
            if k > 1:
                self.waits[h][i]()
                value += self.came[at, k - 2].astype(F32)
            self.out[at, k - 1] = value.astype(BF16)
            self.waits[h][i] = self.links.copy(
                self.out.at[at, k - 1], self.came.at[at, k - 1], self.place.along_seq(sign)
            )

    def result(self, h):
        value = self.term(0, self.rows(h))
        for i in range(2):
            self.waits[h][i]()
            value += self.came[2 * h + i, self.reach(h, i) - 1].astype(F32)
        return value


def layer_kernel(
    sizes, heads, pair, total, tok, wq, wkv, cot, acc_q, acc_kv, seg, span, counts,
    ctx_out, gt_out, out_q_out, out_kv_out,
    ctx, gt, out_q, out_kv, xb, x2, wqbs, wkvb, kvb, cotb, qb, qt, ut, bias, s_buf, e_buf, o_acc, dq_acc, dk_acc, dkvb, sib,
    dq, dqt, dkv, dkvt, gt_sum, rq_send, rq_recv, r_send, r_recv, y_send, y_recv, back_q, back_q_in, back_kv, back_kv_in,
    cyc_q, cyc_kv, send, recv, local,
):
    place = Place(*sizes)
    links = Links(send, recv)
    n_tensor = sizes[2]
    chips, half = place.chips, place.chips // 2
    per = chips // n_tensor
    rows = tok.shape[0]
    krows, kcols = wkv.shape
    hs = kcols // 2
    groups = heads // pair
    pcols = pair * hs
    c = place.core
    sub, rsub = krows // 2, rows // 2
    wqb = [wqbs.at[g] for g in range(groups)]

    own_tok = pltpu.make_async_copy(tok, xb.at[place.t], local.at[0])
    own_tok.start()
    own_cot = pltpu.make_async_copy(cot, cotb, local.at[1])
    own_cot.start()
    greeted = place.greet()

    me = 2 * place.chip + c
    slots = span.shape[2]
    seg_all = seg[...]
    seg_q = seg[:, pl.ds(pl.multiple_of(me * rows, rows), rows)]
    lane = lax.broadcasted_iota(jnp.int32, (1, rows), 1)
    qpos = me * rows + lane
    lo = jnp.zeros((1, rows), jnp.int32)
    hi = jnp.zeros((1, rows), jnp.int32)
    begin = jnp.zeros((1, 1), jnp.int32)
    for s in range(slots):
        end = jnp.sum((seg_all <= s).astype(F32), axis=1, keepdims=True).astype(jnp.int32)
        first, last = span[0, 0, s], span[0, 1, s]
        here = seg_q == s
        inside = (qpos >= first) & (qpos < last)
        lo = jnp.where(here, begin, lo)
        hi = jnp.where(here, jnp.where(inside, jnp.minimum(last, end), qpos + 1), hi)
        begin = end
    valid_t = lane < counts[0, me]
    row = lax.broadcasted_iota(jnp.int32, (rows, rows), 0)
    for d in range(chips):
        for core in range(2):
            b = 2 * place.at(d) + core
            low, high = lo - b * rows, jnp.minimum(hi - b * rows, counts[0, b])
            bias[2 * place.slot(d) + core] = jnp.where((row >= low) & (row < high), 0.0, MASKED)
    greeted()

    ahead = place.along_blk(1)
    halves = (pl.ds(0, sub), pl.ds(sub, sub))
    shift_kv = [links.copy(wkv.at[h], wkvb.at[place.chip, c, h], ahead) for h in halves]
    rhalves = (pl.ds(0, rsub), pl.ds(rsub, rsub))
    near = [[None, None], [None, None]]
    for first in range(2):
        for i, sign in enumerate((1, -1)):
            h = i if first == 0 else 1 - i
            near[i][h] = links.copy(
                tok.at[rhalves[h]], xb.at[place.t, rhalves[h]], place.along_tensor(sign),
                xb.at[place.tensor_at(-sign), rhalves[h]],
            )
    shift_q = [
        links.copy(wq.at[:, pl.ds(p * pcols, pcols)], wqb[p].at[place.chip, c], ahead)
        for p in range(groups)
    ]

    g_wkv = Gather(place, links, wkvb)
    g_wq = [Gather(place, links, buf) for buf in wqb]
    g_kv = Gather(place, links, kvb, by_distance=True)

    later = []

    counts_of = iter(FILLS)

    def fill(n=None):
        for _ in range(next(counts_of) if n is None else n):
            if later:
                later.pop(0)()

    def both(ring, move="advance"):
        for h in range(2):
            getattr(ring, move)(h)

    def first_share(p):
        shift_q[p]()
        g_wq[p].share(0)
        g_wq[p].start(0)

    for p in range(groups):
        later.append(functools.partial(first_share, p))
        later.append(functools.partial(g_wq[p].start, 1))
        for _ in range(half):
            later.append(functools.partial(g_wq[p].advance, 0))
            later.append(functools.partial(g_wq[p].advance, 1))

    for h in range(2):
        shift_kv[h]()
        g_wkv.start(h)
    g_wkv.share(0)
    both(g_wkv)
    fill()
    far = []
    for i, sign in enumerate((1, -1)):
        near[i][i]()
        src = xb.at[place.tensor_at(-sign), rhalves[i]]
        far.append(links.copy(
            src, src, place.along_tensor(sign), xb.at[place.tensor_at(-2 * sign), rhalves[i]]
        ))
    fill()

    both(g_wkv)
    fill()
    both(g_wkv)
    fill()
    own_cot.wait()
    for h in range(heads):
        u = cotb[:, h * hs:(h + 1) * hs].T
        ut[h] = jnp.where(valid_t, u.astype(F32), 0.0).astype(BF16)
    fill()
    both(g_wkv)
    fill()
    for i in range(2):
        near[i][1 - i]()
        far[i]()
    own_tok.wait()
    g_wkv.collect()

    def project(buf):
        out = None
        for t in range(n_tensor):
            part = buf[t * per:(t + 1) * per].reshape(2 * per * krows, buf.shape[3])
            term = matmul(xb[t], part)
            out = term if out is None else out + term
        return out.astype(BF16)

    kvb[place.slot(0), c] = project(wkvb)
    both(g_kv, "start")
    g_kv.share(0)
    fill()
    saves = []

    def save(src, dst):
        saves.append(pltpu.make_async_copy(src, dst, local.at[2 + len(saves)]))
        saves[-1].start()

    got_cyc = [links.copy(acc_q, cyc_q, ahead), links.copy(acc_kv, cyc_kv, ahead)]

    x_got = []

    def own_columns(t):
        for p in range(per):
            mine = pl.ds(pl.multiple_of((2 * p + c) * krows, krows), krows)
            x2[t * per + p, :rows] = xb[t, :, mine]

    def share_columns():
        for z in range(chips):
            t, p = z // per, z % per
            other = pl.ds(pl.multiple_of((2 * p + 1 - c) * krows, krows), krows)
            x_got.append(links.copy(xb.at[t, :, other], x2.at[z, pl.ds(rows, rows)], place.sibling))

    def queries(p):
        while not g_wq[p].finished:
            fill(1)
        g_wq[p].collect()
        qb[p] = project(wqb[p])
        for i in range(pair):
            qt[pair * p + i] = qb[p, :, i * hs:(i + 1) * hs].T

    def rows8(x, op):
        return op(x.reshape(x.shape[0] // 8, 8, rows), axis=0)

    scale = hs ** -0.5
    n_keys = chips * rows

    def look(p, part, tops):
        z = slice(part * half, (part + 1) * half)
        b = slice(part * chips, (part + 1) * chips)
        key = kvb[z, :, :, :hs].reshape(n_keys, hs)
        found = []
        for i in range(pair):
            s = matmul(key, qt[pair * p + i]) + bias[b].reshape(n_keys, rows)
            s_buf[i, part] = s
            found.append(jnp.maximum(tops[i], rows8(s, jnp.max)))
        return found

    for step in range(half):
        if step == half - 1:
            queries(0)
            g_kv.collect(2 * half - 3)
            tops = look(0, 1, [jnp.full((8, rows), MASKED, F32)] * pair)
        else:
            for t in range(step, n_tensor, half - 1):
                own_columns(t)
        fill()
        both(g_kv)
        fill()
    g_kv.collect()
    share_columns()

    def attend(p, tops=None):
        last = p == groups - 1

        def tick(enough=False):
            if not enough:
                fill()

        if tops is None:
            tops = look(p, 1, [jnp.full((8, rows), MASKED, F32)] * pair)
        tick()
        tops = look(p, 0, tops)
        tick()
        tops = [jnp.max(t, axis=0, keepdims=True) * (scale * LOG2E) for t in tops]
        sums = [jnp.zeros((8, rows), F32)] * pair
        for part in range(2):
            z = slice(part * half, (part + 1) * half)
            for i in range(pair):
                e = jnp.exp2(s_buf[i, part] * (scale * LOG2E) - tops[i])
                sums[i] = sums[i] + rows8(e, jnp.sum)
                e = e.astype(BF16)
                e_buf[i, part] = e
                term = matmul(kvb[z, :, :, hs:].reshape(n_keys, hs).T, e)
                o_acc[i] = term if part == 0 else o_acc[i] + term
            tick()
        us, deltas = [], []
        for i in range(pair):
            h = pair * p + i
            inverse = 1.0 / jnp.sum(sums[i], axis=0, keepdims=True)
            attended = jnp.where(valid_t, o_acc[i] * inverse, 0.0)
            ctx[:, h * hs:(h + 1) * hs] = attended.T.astype(BF16)
            u = ut[h].astype(F32) * inverse
            deltas.append(jnp.sum(u * attended, axis=0, keepdims=True))
            ut[h] = u.astype(BF16)
            us.append(u.T.astype(BF16))
        for part in range(2):
            z = slice(part * half, (part + 1) * half)
            dkey = dval = None
            for i in range(pair):
                h = pair * p + i
                e = e_buf[i, part]
                dp = matmul(kvb[z, :, :, hs:].reshape(n_keys, hs), ut[h])
                ds = (e.astype(F32) * (dp - deltas[i])).astype(BF16)
                term = matmul(kvb[z, :, :, :hs].reshape(n_keys, hs).T, ds)
                dq_acc[i] = term if part == 0 else dq_acc[i] + term
                k_term = matmul(ds, qb[p, :, i * hs:(i + 1) * hs])
                v_term = matmul(e, us[i])
                dkey = k_term if dkey is None else dkey + k_term
                dval = v_term if dval is None else dval + v_term
            if p > 0:
                dkey += dk_acc[part, :, :hs]
                dval += dk_acc[part, :, hs:]
            if last:
                dkvb[z, :, :, :hs] = (dkey * scale).astype(BF16).reshape(half, 2, rows, hs)
                dkvb[z, :, :, hs:] = dval.astype(BF16).reshape(half, 2, rows, hs)
                zz = pl.ds(part * half, half)
                exchanged.append(links.copy(dkvb.at[zz, 1 - c], sib.at[zz], place.sibling))
            else:
                dk_acc[part, :, :hs] = dkey
                dk_acc[part, :, hs:] = dval
            tick(part == 1)
        for i in range(pair):
            dqt[p, i * hs:(i + 1) * hs, :rows] = (dq_acc[i] * scale).astype(BF16)
        mine = dqt.at[p, :, pl.ds(0, rows)]
        got_dq = links.copy(mine, dqt.at[p, :, pl.ds(rows, rows)], place.sibling)
        for i in range(pair):
            dq[p, :, i * hs:(i + 1) * hs] = (dq_acc[i] * scale).T.astype(BF16)

        def first_step():
            got_dq()
            s_q[p].step(0)

        later.append(first_step)
        later.append(functools.partial(s_q[p].step, 1))
        for _ in range(half - 1):
            later.append(functools.partial(s_q[p].step, 0))
            later.append(functools.partial(s_q[p].step, 1))
        later.append(functools.partial(hand_back, s_q[p], back_q.at[p], back_q_in.at[p], 0))
        later.append(functools.partial(hand_back, s_q[p], back_q.at[p], back_q_in.at[p], 1))

    exchanged = []

    def fresh_term(grads):
        return lambda d, part: matmul(grads[part], x2[place.at(d)])

    def kv_term(d, part):
        here = place.slot(d)
        return dkvb[here, c, part].astype(F32) + sib[here, part].astype(F32)

    s_q = [
        Scatter(place, links, fresh_term(dqt.at[p]), rq_send.at[p], rq_recv.at[p]) for p in range(groups)
    ]
    s_kv = Scatter(place, links, kv_term, r_send.at[0], r_recv.at[0])
    s_k = Scatter(place, links, fresh_term(dkvt), r_send.at[1], r_recv.at[1])
    got_back = {}

    def hand_back(scatter, out, came, h):
        part = pl.ds(h * sub, sub)
        out[part] = (scatter.result(h) / total).astype(BF16)
        got_back[scatter, h] = links.copy(out.at[part], came.at[part], place.along_blk(-1))

    attend(0, tops)
    for wait in x_got:
        wait()
    for p in range(1, groups):
        queries(p)
        fill()
        attend(p)
    save(ctx, ctx_out)
    shares = (2, 1, -1, 0)
    shard = 2 * per * krows

    def add_queries(i):
        t = place.tensor_at(shares[i])
        value = None
        for p in range(groups):
            term = matmul_t(dq[p], wqb[p][pl.ds(t * per, per)].reshape(shard, pcols))
            value = term if value is None else value + term
        gt_sum[i] = value

    def add_keyval(i):
        t = place.tensor_at(shares[i])
        gt_sum[i] += matmul_t(dkv[...], wkvb[pl.ds(t * per, per)].reshape(shard, kcols))

    for step in range(half):
        if step < 2:
            exchanged[step]()
        both(s_kv, "step")
        fill()
        for i in range(step, len(shares), half):
            add_queries(i)
    for h in range(2):
        value = s_kv.result(h)
        dkv[h * rsub:(h + 1) * rsub] = value.astype(BF16)
        dkvt[:, h * rsub:(h + 1) * rsub] = value.T.astype(BF16)
    got_dkv = links.copy(dkvt.at[:, pl.ds(0, rows)], dkvt.at[:, pl.ds(rows, rows)], place.sibling)

    def row_half(h):
        return slice(h * rsub, (h + 1) * rsub)

    y_far, y_near = [], [[None, None], [None, None]]
    add_keyval(0)
    for i, sign in enumerate((1, -1)):
        y_send[i, 0] = gt_sum[0, row_half(i)].astype(BF16)
        y_far.append(links.copy(y_send.at[i, 0], y_recv.at[i, 0], place.along_tensor(sign)))
    got_dkv()
    both(s_k, "step")
    for i, sign in enumerate((1, -1)):
        add_keyval(1 + i)
        y_send[i, 1] = gt_sum[1 + i, row_half(1 - i)].astype(BF16)
        y_near[i][1 - i] = links.copy(y_send.at[i, 1], y_recv.at[i, 1], place.along_tensor(sign))
    fill()
    both(s_k, "step")
    fill()
    for i, sign in enumerate((1, -1)):
        y_far[i]()
        y_send[i, 2] = (gt_sum[1 + i, row_half(i)] + y_recv[i, 0].astype(F32)).astype(BF16)
        y_near[i][i] = links.copy(y_send.at[i, 2], y_recv.at[i, 2], place.along_tensor(sign))
    add_keyval(3)
    fill()
    for _ in range(half - 2):
        both(s_k, "step")
        fill()
    for h in range(2):
        hand_back(s_k, back_kv, back_kv_in, h)
    fill(len(later))
    for h in range(2):
        value = gt_sum[3, row_half(h)]
        for i in range(2):
            y_near[i][h]()
            value += y_recv[i, 2 if h == i else 1].astype(F32)
        gt[row_half(h)] = value.astype(BF16)
    save(gt, gt_out)
    for wait in got_cyc:
        wait()
    for p in range(groups):
        for h in range(2):
            got_back[s_q[p], h]()
        cols = slice(p * pcols, (p + 1) * pcols)
        out_q[:, cols] = cyc_q[:, cols] + back_q_in[p].astype(F32).T
    save(out_q, out_q_out)
    for h in range(2):
        got_back[s_k, h]()
        out_kv[:, h, :] = cyc_kv[:, h, :] + back_kv_in[h * hs:(h + 1) * hs].astype(F32).T
    save(out_kv, out_kv_out)
    links.drain()
    for made in saves:
        made.wait()


def layer(sizes, heads, pair, tok, wq, wkv, cot, acc_q, acc_kv, seg, span, counts):
    n_blk, n_seq, n_tensor = sizes
    chips = n_seq // 2
    half = chips // 2
    rows, width = tok.shape
    krows, qcols = wq.shape
    kcols = wkv.shape[1]
    hs = kcols // 2
    groups = heads // pair
    pcols = pair * hs
    n_keys = chips * rows
    sub, rsub = krows // 2, rows // 2
    hbm = pl.BlockSpec(memory_space=pl.ANY)
    vmem = pl.BlockSpec(memory_space=pltpu.VMEM)
    smem = pl.BlockSpec(memory_space=pltpu.SMEM)

    def weights(cols):
        return pltpu.VMEM((chips, 2, krows, cols), BF16)

    outs = [
        jax.ShapeDtypeStruct((rows, qcols), BF16),
        jax.ShapeDtypeStruct((rows, width), BF16),
        jax.ShapeDtypeStruct((krows, qcols), F32),
        jax.ShapeDtypeStruct((krows, 2, hs), F32),
    ]
    scratch = [pltpu.VMEM(out.shape, out.dtype) for out in outs] + [
        pltpu.VMEM((n_tensor, rows, width), BF16),
        pltpu.VMEM((chips, 2 * rows, krows), BF16),
        pltpu.VMEM((groups, chips, 2, krows, pcols), BF16),
        weights(kcols),
        pltpu.VMEM((chips, 2, rows, kcols), BF16),
        pltpu.VMEM((rows, qcols), BF16),
        pltpu.VMEM((groups, rows, pcols), BF16),
        pltpu.VMEM((heads, hs, rows), BF16),
        pltpu.VMEM((heads, hs, rows), BF16),
        pltpu.VMEM((n_seq, rows, rows), F32),
        pltpu.VMEM((pair, 2, n_keys, rows), F32),
        pltpu.VMEM((pair, 2, n_keys, rows), BF16),
        pltpu.VMEM((pair, hs, rows), F32),
        pltpu.VMEM((pair, hs, rows), F32),
        pltpu.VMEM((2, n_keys, kcols), F32),
        pltpu.VMEM((chips, 2, rows, kcols), BF16),
        pltpu.VMEM((chips, rows, kcols), BF16),
        pltpu.VMEM((groups, rows, pcols), BF16),
        pltpu.VMEM((groups, pcols, 2 * rows), BF16),
        pltpu.VMEM((rows, kcols), BF16),
        pltpu.VMEM((kcols, 2 * rows), BF16),
        pltpu.VMEM((4, rows, width), F32),
        pltpu.VMEM((groups, 4, half, sub, pcols), BF16),
        pltpu.VMEM((groups, 4, half, sub, pcols), BF16),
        pltpu.VMEM((2, 4, half, sub, kcols), BF16),
        pltpu.VMEM((2, 4, half, sub, kcols), BF16),
        pltpu.VMEM((2, 3, rsub, width), BF16),
        pltpu.VMEM((2, 3, rsub, width), BF16),
        pltpu.VMEM((groups, pcols, krows), BF16),
        pltpu.VMEM((groups, pcols, krows), BF16),
        pltpu.VMEM((kcols, krows), BF16),
        pltpu.VMEM((kcols, krows), BF16),
        pltpu.VMEM((krows, qcols), F32),
        pltpu.VMEM((krows, 2, hs), F32),
        pltpu.SemaphoreType.DMA((256,)),
        pltpu.SemaphoreType.DMA((256,)),
        pltpu.SemaphoreType.DMA((6,)),
    ]
    return pl.pallas_call(
        functools.partial(layer_kernel, sizes, heads, pair, rows * n_seq),
        out_shape=outs,
        in_specs=[hbm] * 6 + [vmem, smem, smem],
        out_specs=[hbm] * 4,
        scratch_shapes=scratch,
        compiler_params=pltpu.CompilerParams(
            collective_id=0, has_side_effects=True, vmem_limit_bytes=62 * MIB
        ),
        name="layer",
    )(tok, wq, wkv, cot, acc_q, acc_kv, seg, span, counts)


def hand_over_kernel(count, *refs):
    sems = refs[-1]
    moves = [pltpu.make_async_copy(refs[i], refs[count + i], sems.at[i]) for i in range(count)]
    for move in moves:
        move.start()
    for move in moves:
        move.wait()


def hand_over(*arrays):
    count = len(arrays)
    hbm = pl.BlockSpec(memory_space=pl.ANY)
    return pl.pallas_call(
        functools.partial(hand_over_kernel, count),
        out_shape=[jax.ShapeDtypeStruct(a.shape, a.dtype) for a in arrays],
        in_specs=[pl.BlockSpec(memory_space=pltpu.VMEM)] * count,
        out_specs=[hbm] * count,
        scratch_shapes=[pltpu.SemaphoreType.DMA((count,))],
        compiler_params=pltpu.CompilerParams(vmem_limit_bytes=60 * MIB),
        name="hand_over",
    )(*arrays)


def on_device(
    sizes, tokens, w_query, w_keyval, accum_query, accum_keyval, cotangent, seg_ids, spans, counts
):
    krows, qcols = w_query.shape[1:]
    groups, kv_cols = w_keyval.shape[2:]
    kcols = groups * kv_cols
    context, grad_tokens, out_q, out_kv = layer(
        sizes, qcols // (kv_cols // 2), PAIR, tokens[0], w_query[0], w_keyval[0].reshape(krows, kcols),
        cotangent[0], accum_query[0], accum_keyval[0].reshape(krows, 2, kcols // 2), seg_ids, jnp.swapaxes(spans, 1, 2), counts,
    )
    context, grad_tokens, out_q, out_kv = hand_over(context, grad_tokens, out_q, out_kv)
    return context[None], grad_tokens[None], out_q[None], out_kv.reshape(w_keyval.shape)


def solution(mesh):
    sizes = (mesh.shape["blk"], mesh.shape["seq"], mesh.shape["tensor"])
    in_specs = (
        P("blk", "seq", "tensor"),
        P("blk", "seq", "tensor"),
        P("blk", "seq", "tensor", None),
        P("blk", "seq", "tensor"),
        P("blk", "seq", "tensor", None),
        P("blk", "seq", "tensor"),
        P("blk", None),
        P("blk", None, None),
        P("blk", None),
    )
    out_specs = (
        P("blk", "seq", "tensor"),
        P("blk", "seq", "tensor"),
        P("blk", "seq", "tensor"),
        P("blk", "seq", "tensor", None),
    )
    return jax.shard_map(
        functools.partial(on_device, sizes), mesh=mesh, in_specs=in_specs, out_specs=out_specs, check_vma=False
    )
```

```python
import functools

import jax
import jax.numpy as jnp
from jax import lax
from jax.experimental import pallas as pl
from jax.experimental.pallas import tpu as pltpu
from jax.sharding import PartitionSpec as P

MESH = pl.DeviceIdType.MESH
BF16 = jnp.bfloat16
F32 = jnp.float32
MIB = 1 << 20
LOG2E = 1.4426950408889634
MASKED = -1e30
PAIR = 2
FILLS = (0, 1, 2, 0, 2, 1, 0, 2, 1, 2, 1, 0, 1, 0, 2, 0, 1, 1, 1, 2, 1, 1, 1, 1, 1, 2, 2, 2, 2, 1, 1, 1, 1, 1, 1)


def matmul(a, b):
    return jnp.dot(a, b, preferred_element_type=F32)


def matmul_t(a, b):
    return lax.dot_general(a, b, (((1,), (1,)), ((), ())), preferred_element_type=F32)


class Place:
    def __init__(self, n_blk, n_seq, n_tensor):
        self.n_blk, self.chips, self.n_tensor = n_blk, n_seq // 2, n_tensor
        me = lax.axis_index("seq")
        self.core, self.chip = lax.rem(me, 2), lax.div(me, 2)
        self.blk, self.t = lax.axis_index("blk"), lax.axis_index("tensor")
        self.sibling = {"seq": me + 1 - 2 * self.core}

    def at(self, distance):
        return lax.rem(self.chip + distance + self.chips, self.chips)

    def slot(self, distance):
        return (distance - self.chips // 4) % self.chips

    def along_seq(self, distance):
        return {"seq": 2 * self.at(distance) + self.core}

    def along_blk(self, distance):
        return {"blk": lax.rem(self.blk + distance + self.n_blk, self.n_blk)}

    def tensor_at(self, distance):
        return lax.rem(self.t + distance + self.n_tensor, self.n_tensor)

    def along_tensor(self, distance):
        return {"tensor": self.tensor_at(distance)}

    def greet(self):
        barrier = pltpu.get_barrier_semaphore()
        others = [self.sibling]
        for sign in (1, -1):
            others += [self.along_seq(sign), self.along_blk(sign), self.along_tensor(sign)]
        for other in others:
            pl.semaphore_signal(barrier, inc=1, device_id=other, device_id_type=MESH)
        return lambda: pl.semaphore_wait(barrier, len(others))


class Links:
    def __init__(self, send, recv):
        self.send, self.recv, self.used, self.sent = send, recv, 0, []

    def copy(self, src, dst, to, arrives=None):
        i = self.used
        self.used += 1
        made = pltpu.make_async_remote_copy(
            src_ref=src, dst_ref=dst, send_sem=self.send.at[i], recv_sem=self.recv.at[i],
            device_id=to, device_id_type=MESH,
        )
        landing = made
        if arrives is not None:
            landing = pltpu.make_async_remote_copy(
                src_ref=arrives, dst_ref=arrives, send_sem=self.send.at[i], recv_sem=self.recv.at[i],
                device_id=to, device_id_type=MESH,
            )
        made.start()
        self.sent.append(made)
        return landing.wait_recv

    def drain(self):
        for made in self.sent:
            made.wait_send()


class Gather:
    def __init__(self, place, links, buf, by_distance=False):
        self.place, self.links, self.buf = place, links, buf
        self.by_distance = by_distance
        self.slot = place.slot if by_distance else place.at
        self.half = place.chips // 2
        sub = buf.shape[2] // 2
        self.parts = (pl.ds(0, sub), pl.ds(sub, sub))
        self.done, self.waits, self.shares, self.finished, self.taken = [0, 0], [None, None], [], False, 0

    def start(self, h):
        place, c = self.place, self.place.core
        self.done[h] = step = self.done[h] + 1
        self.waits[h] = []
        for i, sign in enumerate((1, -1)):
            if step == self.half and i != h:
                continue
            src = self.buf.at[self.slot(-sign * (step - 1)), c, self.parts[h]]
            lands = self.buf.at[self.slot(-sign * step), c, self.parts[h]]
            there = lands if self.by_distance else src
            self.waits[h].append(self.links.copy(src, there, place.along_seq(sign), lands))

    def share(self, distance):
        place = self.place
        src = self.buf.at[self.slot(distance), place.core]
        lands = self.buf.at[self.slot(distance), 1 - place.core]
        self.shares.append(self.links.copy(src, src, place.sibling, lands))

    def advance(self, h):
        step = self.done[h]
        for wait in self.waits[h]:
            wait()
        if step < self.half:
            self.start(h)
        if h == 1:
            self.finished = step == self.half
            for distance in (step, -step) if step < self.half else (step,):
                self.share(distance)

    def collect(self, count=None):
        shares = self.shares[self.taken:count]
        self.taken += len(shares)
        for wait in shares:
            wait()


class Scatter:
    def __init__(self, place, links, term, out, came):
        self.place, self.links, self.term, self.out, self.came = place, links, term, out, came
        self.half = place.chips // 2
        self.sub = out.shape[2]
        self.done, self.waits = [0, 0], [[None, None], [None, None]]

    def rows(self, h):
        return slice(h * self.sub, (h + 1) * self.sub)

    def reach(self, h, i):
        return self.half if h == i else self.half - 1

    def step(self, h):
        self.done[h] = k = self.done[h] + 1
        for i, sign in enumerate((1, -1)):
            n = self.reach(h, i)
            if k > n:
                continue
            at = 2 * h + i
            value = self.term(sign * (n - k + 1), self.rows(h))
            if k > 1:
                self.waits[h][i]()
                value += self.came[at, k - 2].astype(F32)
            self.out[at, k - 1] = value.astype(BF16)
            self.waits[h][i] = self.links.copy(
                self.out.at[at, k - 1], self.came.at[at, k - 1], self.place.along_seq(sign)
            )

    def result(self, h):
        value = self.term(0, self.rows(h))
        for i in range(2):
            self.waits[h][i]()
            value += self.came[2 * h + i, self.reach(h, i) - 1].astype(F32)
        return value


def layer_kernel(
    sizes, heads, pair, total, tok, wq, wkv, cot, acc_q, acc_kv, seg, span, counts,
    ctx_out, gt_out, out_q_out, out_kv_out,
    ctx, gt, out_q, out_kv, xb, x2, wqbs, wkvb, kvb, cotb, qb, qt, ut, bias, s_buf, e_buf, o_acc, dq_acc, dk_acc, dkvb, sib,
    dq, dqt, dkv, dkvt, gt_sum, rq_send, rq_recv, r_send, r_recv, y_send, y_recv, back_q, back_q_in, back_kv, back_kv_in,
    cyc_q, cyc_kv, send, recv, local,
):
    place = Place(*sizes)
    links = Links(send, recv)
    n_tensor = sizes[2]
    chips, half = place.chips, place.chips // 2
    per = chips // n_tensor
    rows = tok.shape[0]
    krows, kcols = wkv.shape
    hs = kcols // 2
    groups = heads // pair
    pcols = pair * hs
    c = place.core
    sub, rsub = krows // 2, rows // 2
    wqb = [wqbs.at[g] for g in range(groups)]

    own_tok = pltpu.make_async_copy(tok, xb.at[place.t], local.at[0])
    own_tok.start()
    own_cot = pltpu.make_async_copy(cot, cotb, local.at[1])
    own_cot.start()
    greeted = place.greet()

    me = 2 * place.chip + c
    slots = span.shape[2]
    seg_all = seg[...]
    seg_q = seg[:, pl.ds(pl.multiple_of(me * rows, rows), rows)]
    lane = lax.broadcasted_iota(jnp.int32, (1, rows), 1)
    qpos = me * rows + lane
    lo = jnp.zeros((1, rows), jnp.int32)
    hi = jnp.zeros((1, rows), jnp.int32)
    begin = jnp.zeros((1, 1), jnp.int32)
    for s in range(slots):
        end = jnp.sum((seg_all <= s).astype(F32), axis=1, keepdims=True).astype(jnp.int32)
        first, last = span[0, 0, s], span[0, 1, s]
        here = seg_q == s
        inside = (qpos >= first) & (qpos < last)
        lo = jnp.where(here, begin, lo)
        hi = jnp.where(here, jnp.where(inside, jnp.minimum(last, end), qpos + 1), hi)
        begin = end
    valid_t = lane < counts[0, me]
    row = lax.broadcasted_iota(jnp.int32, (rows, rows), 0)
    for d in range(chips):
        for core in range(2):
            b = 2 * place.at(d) + core
            low, high = lo - b * rows, jnp.minimum(hi - b * rows, counts[0, b])
            bias[2 * place.slot(d) + core] = jnp.where((row >= low) & (row < high), 0.0, MASKED)
    greeted()

    ahead = place.along_blk(1)
    halves = (pl.ds(0, sub), pl.ds(sub, sub))
    shift_kv = [links.copy(wkv.at[h], wkvb.at[place.chip, c, h], ahead) for h in halves]
    rhalves = (pl.ds(0, rsub), pl.ds(rsub, rsub))
    near = [[None, None], [None, None]]
    for first in range(2):
        for i, sign in enumerate((1, -1)):
            h = i if first == 0 else 1 - i
            near[i][h] = links.copy(
                tok.at[rhalves[h]], xb.at[place.t, rhalves[h]], place.along_tensor(sign),
                xb.at[place.tensor_at(-sign), rhalves[h]],
            )
    shift_q = [
        links.copy(wq.at[:, pl.ds(p * pcols, pcols)], wqb[p].at[place.chip, c], ahead)
        for p in range(groups)
    ]

    g_wkv = Gather(place, links, wkvb)
    g_wq = [Gather(place, links, buf) for buf in wqb]
    g_kv = Gather(place, links, kvb, by_distance=True)

    later = []

    counts_of = iter(FILLS)

    def fill(n=None):
        for _ in range(next(counts_of) if n is None else n):
            if later:
                later.pop(0)()

    def both(ring, move="advance"):
        for h in range(2):
            getattr(ring, move)(h)

    def first_share(p):
        shift_q[p]()
        g_wq[p].share(0)
        g_wq[p].start(0)

    for p in range(groups):
        later.append(functools.partial(first_share, p))
        later.append(functools.partial(g_wq[p].start, 1))
        for _ in range(half):
            later.append(functools.partial(g_wq[p].advance, 0))
            later.append(functools.partial(g_wq[p].advance, 1))

    for h in range(2):
        shift_kv[h]()
        g_wkv.start(h)
    g_wkv.share(0)
    both(g_wkv)
    fill()
    far = []
    for i, sign in enumerate((1, -1)):
        near[i][i]()
        src = xb.at[place.tensor_at(-sign), rhalves[i]]
        far.append(links.copy(
            src, src, place.along_tensor(sign), xb.at[place.tensor_at(-2 * sign), rhalves[i]]
        ))
    fill()

    both(g_wkv)
    fill()
    both(g_wkv)
    fill()
    own_cot.wait()
    for h in range(heads):
        u = cotb[:, h * hs:(h + 1) * hs].T
        ut[h] = jnp.where(valid_t, u.astype(F32), 0.0).astype(BF16)
    fill()
    both(g_wkv)
    fill()
    for i in range(2):
        near[i][1 - i]()
        far[i]()
    own_tok.wait()
    g_wkv.collect()

    def project(buf):
        out = None
        for t in range(n_tensor):
            part = buf[t * per:(t + 1) * per].reshape(2 * per * krows, buf.shape[3])
            term = matmul(xb[t], part)
            out = term if out is None else out + term
        return out.astype(BF16)

    kvb[place.slot(0), c] = project(wkvb)
    both(g_kv, "start")
    g_kv.share(0)
    fill()
    saves = []

    def save(src, dst):
        saves.append(pltpu.make_async_copy(src, dst, local.at[2 + len(saves)]))
        saves[-1].start()

    got_cyc = [links.copy(acc_q, cyc_q, ahead), links.copy(acc_kv, cyc_kv, ahead)]

    x_got = []

    def own_columns(t):
        for p in range(per):
            mine = pl.ds(pl.multiple_of((2 * p + c) * krows, krows), krows)
            x2[t * per + p, :rows] = xb[t, :, mine]

    def share_columns():
        for z in range(chips):
            t, p = z // per, z % per
            other = pl.ds(pl.multiple_of((2 * p + 1 - c) * krows, krows), krows)
            x_got.append(links.copy(xb.at[t, :, other], x2.at[z, pl.ds(rows, rows)], place.sibling))

    def queries(p):
        while not g_wq[p].finished:
            fill(1)
        g_wq[p].collect()
        qb[p] = project(wqb[p])
        for i in range(pair):
            qt[pair * p + i] = qb[p, :, i * hs:(i + 1) * hs].T

    def rows8(x, op):
        return op(x.reshape(x.shape[0] // 8, 8, rows), axis=0)

    scale = hs ** -0.5
    n_keys = chips * rows

    def look(p, part, tops):
        z = slice(part * half, (part + 1) * half)
        b = slice(part * chips, (part + 1) * chips)
        key = kvb[z, :, :, :hs].reshape(n_keys, hs)
        found = []
        for i in range(pair):
            s = matmul(key, qt[pair * p + i]) + bias[b].reshape(n_keys, rows)
            s_buf[i, part] = s
            found.append(jnp.maximum(tops[i], rows8(s, jnp.max)))
        return found

    for step in range(half):
        if step == half - 1:
            queries(0)
            g_kv.collect(2 * half - 3)
            tops = look(0, 1, [jnp.full((8, rows), MASKED, F32)] * pair)
        else:
            for t in range(step, n_tensor, half - 1):
                own_columns(t)
        fill()
        both(g_kv)
        fill()
    g_kv.collect()
    share_columns()

    def attend(p, tops=None):
        last = p == groups - 1

        def tick(enough=False):
            if not enough:
                fill()

        if tops is None:
            tops = look(p, 1, [jnp.full((8, rows), MASKED, F32)] * pair)
        tick()
        tops = look(p, 0, tops)
        tick()
        tops = [jnp.max(t, axis=0, keepdims=True) * (scale * LOG2E) for t in tops]
        sums = [jnp.zeros((8, rows), F32)] * pair
        for part in range(2):
            z = slice(part * half, (part + 1) * half)
            for i in range(pair):
                e = jnp.exp2(s_buf[i, part] * (scale * LOG2E) - tops[i])
                sums[i] = sums[i] + rows8(e, jnp.sum)
                e = e.astype(BF16)
                e_buf[i, part] = e
                term = matmul(kvb[z, :, :, hs:].reshape(n_keys, hs).T, e)
                o_acc[i] = term if part == 0 else o_acc[i] + term
            tick()
        us, deltas = [], []
        for i in range(pair):
            h = pair * p + i
            inverse = 1.0 / jnp.sum(sums[i], axis=0, keepdims=True)
            attended = jnp.where(valid_t, o_acc[i] * inverse, 0.0)
            ctx[:, h * hs:(h + 1) * hs] = attended.T.astype(BF16)
            u = ut[h].astype(F32) * inverse
            deltas.append(jnp.sum(u * attended, axis=0, keepdims=True))
            ut[h] = u.astype(BF16)
            us.append(u.T.astype(BF16))
        for part in range(2):
            z = slice(part * half, (part + 1) * half)
            dkey = dval = None
            for i in range(pair):
                h = pair * p + i
                e = e_buf[i, part]
                dp = matmul(kvb[z, :, :, hs:].reshape(n_keys, hs), ut[h])
                ds = (e.astype(F32) * (dp - deltas[i])).astype(BF16)
                term = matmul(kvb[z, :, :, :hs].reshape(n_keys, hs).T, ds)
                dq_acc[i] = term if part == 0 else dq_acc[i] + term
                k_term = matmul(ds, qb[p, :, i * hs:(i + 1) * hs])
                v_term = matmul(e, us[i])
                dkey = k_term if dkey is None else dkey + k_term
                dval = v_term if dval is None else dval + v_term
            if p > 0:
                dkey += dk_acc[part, :, :hs]
                dval += dk_acc[part, :, hs:]
            if last:
                dkvb[z, :, :, :hs] = (dkey * scale).astype(BF16).reshape(half, 2, rows, hs)
                dkvb[z, :, :, hs:] = dval.astype(BF16).reshape(half, 2, rows, hs)
                zz = pl.ds(part * half, half)
                exchanged.append(links.copy(dkvb.at[zz, 1 - c], sib.at[zz], place.sibling))
            else:
                dk_acc[part, :, :hs] = dkey
                dk_acc[part, :, hs:] = dval
            tick(part == 1)
        for i in range(pair):
            dqt[p, i * hs:(i + 1) * hs, :rows] = (dq_acc[i] * scale).astype(BF16)
        mine = dqt.at[p, :, pl.ds(0, rows)]
        got_dq = links.copy(mine, dqt.at[p, :, pl.ds(rows, rows)], place.sibling)
        for i in range(pair):
            dq[p, :, i * hs:(i + 1) * hs] = (dq_acc[i] * scale).T.astype(BF16)

        def first_step():
            got_dq()
            s_q[p].step(0)

        later.append(first_step)
        later.append(functools.partial(s_q[p].step, 1))
        for _ in range(half - 1):
            later.append(functools.partial(s_q[p].step, 0))
            later.append(functools.partial(s_q[p].step, 1))
        later.append(functools.partial(hand_back, s_q[p], back_q.at[p], back_q_in.at[p], 0))
        later.append(functools.partial(hand_back, s_q[p], back_q.at[p], back_q_in.at[p], 1))

    exchanged = []

    def fresh_term(grads):
        return lambda d, part: matmul(grads[part], x2[place.at(d)])

    def kv_term(d, part):
        here = place.slot(d)
        return dkvb[here, c, part].astype(F32) + sib[here, part].astype(F32)

    s_q = [
        Scatter(place, links, fresh_term(dqt.at[p]), rq_send.at[p], rq_recv.at[p]) for p in range(groups)
    ]
    s_kv = Scatter(place, links, kv_term, r_send.at[0], r_recv.at[0])
    s_k = Scatter(place, links, fresh_term(dkvt), r_send.at[1], r_recv.at[1])
    got_back = {}

    def hand_back(scatter, out, came, h):
        part = pl.ds(h * sub, sub)
        out[part] = (scatter.result(h) / total).astype(BF16)
        got_back[scatter, h] = links.copy(out.at[part], came.at[part], place.along_blk(-1))

    attend(0, tops)
    for wait in x_got:
        wait()
    for p in range(1, groups):
        queries(p)
        fill()
        attend(p)
    save(ctx, ctx_out)
    shares = (2, 1, -1, 0)
    shard = 2 * per * krows

    def add_queries(i):
        t = place.tensor_at(shares[i])
        value = None
        for p in range(groups):
            term = matmul_t(dq[p], wqb[p][pl.ds(t * per, per)].reshape(shard, pcols))
            value = term if value is None else value + term
        gt_sum[i] = value

    def add_keyval(i):
        t = place.tensor_at(shares[i])
        gt_sum[i] += matmul_t(dkv[...], wkvb[pl.ds(t * per, per)].reshape(shard, kcols))

    for step in range(half):
        if step < 2:
            exchanged[step]()
        both(s_kv, "step")
        fill()
        for i in range(step, len(shares), half):
            add_queries(i)
    for h in range(2):
        value = s_kv.result(h)
        dkv[h * rsub:(h + 1) * rsub] = value.astype(BF16)
        dkvt[:, h * rsub:(h + 1) * rsub] = value.T.astype(BF16)
    got_dkv = links.copy(dkvt.at[:, pl.ds(0, rows)], dkvt.at[:, pl.ds(rows, rows)], place.sibling)

    def row_half(h):
        return slice(h * rsub, (h + 1) * rsub)

    y_far, y_near = [], [[None, None], [None, None]]
    add_keyval(0)
    for i, sign in enumerate((1, -1)):
        y_send[i, 0] = gt_sum[0, row_half(i)].astype(BF16)
        y_far.append(links.copy(y_send.at[i, 0], y_recv.at[i, 0], place.along_tensor(sign)))
    got_dkv()
    both(s_k, "step")
    for i, sign in enumerate((1, -1)):
        add_keyval(1 + i)
        y_send[i, 1] = gt_sum[1 + i, row_half(1 - i)].astype(BF16)
        y_near[i][1 - i] = links.copy(y_send.at[i, 1], y_recv.at[i, 1], place.along_tensor(sign))
    fill()
    both(s_k, "step")
    fill()
    for i, sign in enumerate((1, -1)):
        y_far[i]()
        y_send[i, 2] = (gt_sum[1 + i, row_half(i)] + y_recv[i, 0].astype(F32)).astype(BF16)
        y_near[i][i] = links.copy(y_send.at[i, 2], y_recv.at[i, 2], place.along_tensor(sign))
    add_keyval(3)
    fill()
    for _ in range(half - 2):
        both(s_k, "step")
        fill()
    for h in range(2):
        hand_back(s_k, back_kv, back_kv_in, h)
    fill(len(later))
    for h in range(2):
        value = gt_sum[3, row_half(h)]
        for i in range(2):
            y_near[i][h]()
            value += y_recv[i, 2 if h == i else 1].astype(F32)
        gt[row_half(h)] = value.astype(BF16)
    save(gt, gt_out)
    for wait in got_cyc:
        wait()
    for p in range(groups):
        for h in range(2):
            got_back[s_q[p], h]()
        cols = slice(p * pcols, (p + 1) * pcols)
        out_q[:, cols] = cyc_q[:, cols] + back_q_in[p].astype(F32).T
    save(out_q, out_q_out)
    for h in range(2):
        got_back[s_k, h]()
        out_kv[:, h, :] = cyc_kv[:, h, :] + back_kv_in[h * hs:(h + 1) * hs].astype(F32).T
    save(out_kv, out_kv_out)
    links.drain()
    for made in saves:
        made.wait()


def layer(sizes, heads, pair, tok, wq, wkv, cot, acc_q, acc_kv, seg, span, counts):
    n_blk, n_seq, n_tensor = sizes
    chips = n_seq // 2
    half = chips // 2
    rows, width = tok.shape
    krows, qcols = wq.shape
    kcols = wkv.shape[1]
    hs = kcols // 2
    groups = heads // pair
    pcols = pair * hs
    n_keys = chips * rows
    sub, rsub = krows // 2, rows // 2
    hbm = pl.BlockSpec(memory_space=pl.ANY)
    vmem = pl.BlockSpec(memory_space=pltpu.VMEM)
    smem = pl.BlockSpec(memory_space=pltpu.SMEM)

    def weights(cols):
        return pltpu.VMEM((chips, 2, krows, cols), BF16)

    outs = [
        jax.ShapeDtypeStruct((rows, qcols), BF16),
        jax.ShapeDtypeStruct((rows, width), BF16),
        jax.ShapeDtypeStruct((krows, qcols), F32),
        jax.ShapeDtypeStruct((krows, 2, hs), F32),
    ]
    scratch = [pltpu.VMEM(out.shape, out.dtype) for out in outs] + [
        pltpu.VMEM((n_tensor, rows, width), BF16),
        pltpu.VMEM((chips, 2 * rows, krows), BF16),
        pltpu.VMEM((groups, chips, 2, krows, pcols), BF16),
        weights(kcols),
        pltpu.VMEM((chips, 2, rows, kcols), BF16),
        pltpu.VMEM((rows, qcols), BF16),
        pltpu.VMEM((groups, rows, pcols), BF16),
        pltpu.VMEM((heads, hs, rows), BF16),
        pltpu.VMEM((heads, hs, rows), BF16),
        pltpu.VMEM((n_seq, rows, rows), F32),
        pltpu.VMEM((pair, 2, n_keys, rows), F32),
        pltpu.VMEM((pair, 2, n_keys, rows), BF16),
        pltpu.VMEM((pair, hs, rows), F32),
        pltpu.VMEM((pair, hs, rows), F32),
        pltpu.VMEM((2, n_keys, kcols), F32),
        pltpu.VMEM((chips, 2, rows, kcols), BF16),
        pltpu.VMEM((chips, rows, kcols), BF16),
        pltpu.VMEM((groups, rows, pcols), BF16),
        pltpu.VMEM((groups, pcols, 2 * rows), BF16),
        pltpu.VMEM((rows, kcols), BF16),
        pltpu.VMEM((kcols, 2 * rows), BF16),
        pltpu.VMEM((4, rows, width), F32),
        pltpu.VMEM((groups, 4, half, sub, pcols), BF16),
        pltpu.VMEM((groups, 4, half, sub, pcols), BF16),
        pltpu.VMEM((2, 4, half, sub, kcols), BF16),
        pltpu.VMEM((2, 4, half, sub, kcols), BF16),
        pltpu.VMEM((2, 3, rsub, width), BF16),
        pltpu.VMEM((2, 3, rsub, width), BF16),
        pltpu.VMEM((groups, pcols, krows), BF16),
        pltpu.VMEM((groups, pcols, krows), BF16),
        pltpu.VMEM((kcols, krows), BF16),
        pltpu.VMEM((kcols, krows), BF16),
        pltpu.VMEM((krows, qcols), F32),
        pltpu.VMEM((krows, 2, hs), F32),
        pltpu.SemaphoreType.DMA((256,)),
        pltpu.SemaphoreType.DMA((256,)),
        pltpu.SemaphoreType.DMA((6,)),
    ]
    return pl.pallas_call(
        functools.partial(layer_kernel, sizes, heads, pair, rows * n_seq),
        out_shape=outs,
        in_specs=[hbm] * 6 + [vmem, smem, smem],
        out_specs=[hbm] * 4,
        scratch_shapes=scratch,
        compiler_params=pltpu.CompilerParams(
            collective_id=0, has_side_effects=True, vmem_limit_bytes=62 * MIB
        ),
        name="layer",
    )(tok, wq, wkv, cot, acc_q, acc_kv, seg, span, counts)


def hand_over_kernel(count, *refs):
    arrays, results, held, sems = refs[:count], refs[count:2 * count], refs[2 * count:-1], refs[-1]
    comes = [pltpu.make_async_copy(arrays[i], held[i], sems.at[0, i]) for i in range(count)]
    goes = [pltpu.make_async_copy(held[i], results[i], sems.at[1, i]) for i in range(count)]
    for come in comes:
        come.start()
    for come, go in zip(comes, goes):
        come.wait()
        go.start()
    for go in goes:
        go.wait()


def hand_over(*arrays):
    count = len(arrays)
    hbm = pl.BlockSpec(memory_space=pl.ANY)
    return pl.pallas_call(
        functools.partial(hand_over_kernel, count),
        out_shape=[jax.ShapeDtypeStruct(a.shape, a.dtype) for a in arrays],
        in_specs=[hbm] * count,
        out_specs=[hbm] * count,
        scratch_shapes=[pltpu.VMEM(a.shape, a.dtype) for a in arrays] + [pltpu.SemaphoreType.DMA((2, count))],
        compiler_params=pltpu.CompilerParams(vmem_limit_bytes=60 * MIB),
        name="hand_over",
    )(*arrays)


def on_device(
    sizes, tokens, w_query, w_keyval, accum_query, accum_keyval, cotangent, seg_ids, spans, counts
):
    krows, qcols = w_query.shape[1:]
    groups, kv_cols = w_keyval.shape[2:]
    kcols = groups * kv_cols
    context, grad_tokens, out_q, out_kv = layer(
        sizes, qcols // (kv_cols // 2), PAIR, tokens[0], w_query[0], w_keyval[0].reshape(krows, kcols),
        cotangent[0], accum_query[0], accum_keyval[0].reshape(krows, 2, kcols // 2), seg_ids, jnp.swapaxes(spans, 1, 2), counts,
    )
    context, grad_tokens, out_q, out_kv = hand_over(context, grad_tokens, out_q, out_kv)
    return context[None], grad_tokens[None], out_q[None], out_kv.reshape(w_keyval.shape)


def solution(mesh):
    sizes = (mesh.shape["blk"], mesh.shape["seq"], mesh.shape["tensor"])
    in_specs = (
        P("blk", "seq", "tensor"),
        P("blk", "seq", "tensor"),
        P("blk", "seq", "tensor", None),
        P("blk", "seq", "tensor"),
        P("blk", "seq", "tensor", None),
        P("blk", "seq", "tensor"),
        P("blk", None),
        P("blk", None, None),
        P("blk", None),
    )
    out_specs = (
        P("blk", "seq", "tensor"),
        P("blk", "seq", "tensor"),
        P("blk", "seq", "tensor"),
        P("blk", "seq", "tensor", None),
    )
    return jax.shard_map(
        functools.partial(on_device, sizes), mesh=mesh, in_specs=in_specs, out_specs=out_specs, check_vma=False
    )
```
